256 devices in a mesh: row: 8 (over x, z_hi), col: 32 (over z_lo, y, core).
Axes of the slice: x: 4, y: 4, z: 8 (z_hi: 2, z_lo: 4; z = z_hi * 4 + z_lo), core: 2. Of those that a mesh axis runs over, the one named last changes fastest.
Arguments:
- pair_map: bfloat16 [32, 1024, 1024], P(None, 'col', 'row'), may hold values from -6 to 6
- out_grad: bfloat16 [32, 1024, 1024], P(None, 'col', 'row'), may hold values from -6 to 6
- first_a: bfloat16 [3, 3, 32, 32], replicated, may hold values from -0.375 to 0.375
- first_b: bfloat16 [3, 3, 32, 32], replicated, may hold values from -0.375 to 0.375
- second_a: bfloat16 [3, 3, 32, 32], replicated, may hold values from -0.375 to 0.375
- second_b: bfloat16 [3, 3, 32, 32], replicated, may hold values from -0.375 to 0.375
Outputs:
- decoded: bfloat16 [32, 1024, 1024], P(None, 'col', 'row')
- grad_map: bfloat16 [32, 1024, 1024], P(None, 'col', 'row')
- grad_first_a: float32 [3, 3, 32, 32], replicated
- grad_first_b: float32 [3, 3, 32, 32], replicated
- grad_second_a: float32 [3, 3, 32, 32], replicated
- grad_second_b: float32 [3, 3, 32, 32], replicated
The draws below stay inside these ranges and needn't reach their ends.
All inputs are finite; a program needn't handle non-finite values.
Results may differ from the reference program's by a relative error of at most 0.0078.
Values may be sent and summed in bfloat16 or wider, within the bound.
A program may use at most 128 MiB of HBM per device.

```python
import jax
import jax.numpy as jnp
from jax import lax

C = 32
DILATE_ONE = 4
DILATE_TWO = 8
NP = 1024


def block_levels(key, dims, cuts, least, high):
    def one(position, shards_of):
        heights = jax.random.uniform(jax.random.fold_in(jax.random.fold_in(key, 6), position), (shards_of,), jnp.float32, least / len(cuts), high / len(cuts))
        return jnp.repeat(jnp.exp(heights), dims[position] // shards_of).reshape((-1,) + (1,) * (len(dims) - position - 1))

    loudness = one(*cuts[0])
    for cut in cuts[1:]:
        loudness = loudness * one(*cut)
    return loudness


def scatter_about(key, extent, deviation, bound, cuts=(), held_as=jnp.bfloat16):
    loudness = block_levels(key, extent, cuts, -0.22, 0.18) if cuts else 1.0
    values = jax.random.normal(key, extent, jnp.float32) * deviation * loudness
    return jnp.minimum(jnp.maximum(values, -bound), bound).astype(held_as)


def setup_inputs(seed: int = 0) -> dict:
    splits = jax.random.split(jax.random.key(seed), 7)
    pair_map = scatter_about(splits[0], (C, NP, NP), 1.0, 6.0, ((1, 32), (2, 8)))
    out_grad = scatter_about(splits[1], (C, NP, NP), 1.0, 6.0, ((1, 32), (2, 8)))
    first_a = scatter_about(splits[2], (3, 3, C, C), (9 * C) ** -0.5, 0.375)
    first_b = scatter_about(splits[3], (3, 3, C, C), (9 * C) ** -0.5, 0.375)
    second_a = scatter_about(splits[4], (3, 3, C, C), (9 * C) ** -0.5, 0.375)
    second_b = scatter_about(splits[5], (3, 3, C, C), (9 * C) ** -0.5, 0.375)
    return {"pair_map": pair_map, "out_grad": out_grad, "first_a": first_a, "first_b": first_b, "second_a": second_a, "second_b": second_b}


def convolve(source, kernel, spacing):
    left = source.astype(jnp.float32)[None]
    right = jnp.transpose(kernel.astype(jnp.float32), (2, 3, 0, 1))
    result = lax.conv_general_dilated(left, right, (1, 1), [(spacing, spacing), (spacing, spacing)], rhs_dilation=(spacing, spacing), dimension_numbers=('NCHW', 'OIHW', 'NCHW'), precision=lax.Precision.HIGHEST)
    return result[0]

def flipped(kernel):
    return jnp.swapaxes(kernel[::-1, ::-1], 2, 3)

def kernel_grad(source, cotangent, spacing):
    side = source.shape[1]
    padded = jnp.pad(source.astype(jnp.float32), ((0, 0), (spacing, spacing), (spacing, spacing)))
    grads = cotangent.astype(jnp.float32)
    outer = []
    for row_tap in range(3):
        inner = []
        for col_tap in range(3):
            shifted = padded[:, row_tap * spacing:row_tap * spacing + side, col_tap * spacing:col_tap * spacing + side]
            inner.append(jnp.einsum('orc,irc->oi', grads, shifted, precision=lax.Precision.HIGHEST))
        outer.append(jnp.stack(inner))
    return jnp.stack(outer)

def mirrored(field):
    widened = field.astype(jnp.float32)
    return (widened + jnp.swapaxes(widened, 1, 2)) * 0.5

def silu_slope(before):
    sigmoid_value = jax.nn.sigmoid(before)
    return sigmoid_value * (1.0 + before * (1.0 - sigmoid_value))

def reference(pair_map, out_grad, first_a, first_b, second_a, second_b):
    spacings = (DILATE_ONE, DILATE_TWO)
    kernels = ((first_a, first_b), (second_a, second_b))
    current = pair_map
    stored = []
    for block_index in range(2):
        kernel_a, kernel_b = kernels[block_index]
        spacing = spacings[block_index]
        before = convolve(current, kernel_a, spacing)
        hidden = jax.nn.silu(before).astype(jnp.bfloat16)
        summed = (current.astype(jnp.float32) + convolve(hidden, kernel_b, spacing)).astype(jnp.bfloat16)
        stored.append((current, before, hidden))
        current = mirrored(summed).astype(jnp.bfloat16)
    decoded = current
    upstream = out_grad
    kernel_grads = [None, None, None, None]
    for block_index in (1, 0):
        kernel_a, kernel_b = kernels[block_index]
        spacing = spacings[block_index]
        source, before, hidden = stored[block_index]
        averaged = mirrored(upstream).astype(jnp.bfloat16)
        kernel_grads[2 * block_index + 1] = kernel_grad(hidden, averaged, spacing)
        hidden_grad = convolve(averaged, flipped(kernel_b), spacing)
        inner_grad = (hidden_grad * silu_slope(before)).astype(jnp.bfloat16)
        kernel_grads[2 * block_index] = kernel_grad(source, inner_grad, spacing)
        upstream = (averaged.astype(jnp.float32) + convolve(inner_grad, flipped(kernel_a), spacing)).astype(jnp.bfloat16)
    return (decoded, upstream, kernel_grads[0], kernel_grads[1], kernel_grads[2], kernel_grads[3])
```

```python
import functools

import jax
import jax.numpy as jnp
from jax import lax
from jax.experimental import pallas as pl
from jax.experimental.pallas import tpu as pltpu
from jax.sharding import PartitionSpec as P

C = 32
BC = 32
BR = 128
DILATE_ONE = 4
DILATE_TWO = 8
MESH = pl.DeviceIdType.MESH
BF = jnp.bfloat16
F32 = jnp.float32


def dot(a, b):
    return jnp.dot(a, b, preferred_element_type=F32)


def permutation(inverse):
    row = lax.broadcasted_iota(jnp.int32, (256, 256), 0)
    col = lax.broadcasted_iota(jnp.int32, (256, 256), 1)
    if inverse:
        row, col = col, row
    same = (row // 8 == col % 32) & (row % 8 == col // 32)
    return jnp.where(same, 1.0, 0.0).astype(BF)


def fill_matrix(ref, row, kernel, flip, swap):
    for p in range(3):
        for q in range(3):
            a, b = (q, p) if swap else (p, q)
            if flip:
                piece = kernel[2 - a, 2 - b].astype(F32).T.astype(BF)
            else:
                piece = kernel[a, b]
            tap = 3 * p + q
            ref[row : row + C, tap * C : tap * C + C] = piece


def stack_shifts(v, d, lanes):
    return (
        pltpu.roll(v, d, 1)[:, :lanes],
        v[:, :lanes],
        pltpu.roll(v, 2 * BR - d, 1)[:, :lanes],
    )


def put_stack(ref, row, v, d, lanes):
    for q, part in enumerate(stack_shifts(v, d, lanes)):
        ref[row, q * C : q * C + C, :] = part


def taps(ref, row, d):
    return jnp.concatenate([ref[row], ref[row + d], ref[row + 2 * d]], axis=0)


def rows(count, body, unroll=8):
    def step(t, carry):
        for u in range(unroll):
            body(t * unroll + u)
        return carry

    lax.fori_loop(0, count // unroll, step, 0)


class Halo:
    names = ("own", "top", "bottom", "pack", "land", "send", "recv")

    def __init__(self, width, place, refs):
        self.h = width
        self.per = BR // width
        self.edge = 16 // self.per
        self.count = BC // self.per
        self.place = place
        self.own, self.top, self.bottom, self.pack, self.land, self.send, self.recv = refs

    @staticmethod
    def scratch(width):
        per = BR // width
        return [
            pltpu.VMEM((BC, C, BR), BF),
            pltpu.VMEM((width, C, BR), BF),
            pltpu.VMEM((width, C, BR), BF),
            pltpu.VMEM((2, BC // per, C, BR), BF),
            pltpu.VMEM((2, 64 // per, C, BR), BF),
            pltpu.SemaphoreType.DMA((8,)),
            pltpu.SemaphoreType.DMA((8,)),
        ]

    def pieces(self):
        e, n, h = self.edge, self.count, self.h
        return (
            (0, -1, self.own.at[0:h], self.bottom),
            (0, 1, self.own.at[BC - h : BC], self.top),
            (-1, 0, self.pack.at[0], self.land.at[0, e : e + n]),
            (1, 0, self.pack.at[1], self.land.at[1, e : e + n]),
            (-1, -1, self.pack.at[0, 0:e], self.land.at[0, e + n :]),
            (-1, 1, self.pack.at[0, n - e : n], self.land.at[0, 0:e]),
            (1, -1, self.pack.at[1, 0:e], self.land.at[1, e + n :]),
            (1, 1, self.pack.at[1, n - e : n], self.land.at[1, 0:e]),
        )

    def copy(self, k, piece):
        dr, dc, src, dst = piece
        return pltpu.make_async_remote_copy(
            src_ref=src,
            dst_ref=dst,
            send_sem=self.send.at[k],
            recv_sem=self.recv.at[k],
            device_id=(self.place.ri + dr, self.place.ci + dc),
            device_id_type=MESH,
        )

    def fill_edges(self):
        for dr, dc, src, dst in self.pieces():

            @pl.when(jnp.logical_not(self.place.inside(-dr, -dc)))
            def _():
                dst[...] = jnp.zeros(dst.shape, BF)

    def start(self):
        h, per = self.h, self.per
        group = lax.broadcasted_iota(jnp.int32, (C, BR), 1) // h

        def pack(t, carry):
            low = jnp.zeros((C, BR), BF)
            high = jnp.zeros((C, BR), BF)
            for j in range(per):
                v = self.own[t * per + j]
                low = jnp.where(group == j, pltpu.roll(v, j * h, 1), low)
                high = jnp.where(group == j, pltpu.roll(v, (j * h + h) % BR, 1), high)
            self.pack[0, t] = low
            self.pack[1, t] = high
            return carry

        lax.fori_loop(0, self.count, pack, 0)
        for k, piece in enumerate(self.pieces()):

            @pl.when(self.place.inside(piece[0], piece[1]))
            def _():
                self.copy(k, piece).start()

    def wait(self):
        for k, piece in enumerate(self.pieces()):

            @pl.when(self.place.inside(-piece[0], -piece[1]))
            def _():
                self.copy(k, piece).wait_recv()

    def drain(self):
        for k, piece in enumerate(self.pieces()):

            @pl.when(self.place.inside(piece[0], piece[1]))
            def _():
                self.copy(k, piece).wait_send()

    def build(self, ref, d):
        h, per, e = self.h, self.per, self.edge
        lane = lax.broadcasted_iota(jnp.int32, (C, BR), 1)

        def segment(main, first, pack, j0, nj, packs):
            def step(t, carry):
                low = self.land[0, pack + t]
                high = self.land[1, pack + t]
                for u in range(nj):
                    j = j0 + u
                    row = t * nj + u
                    side = jnp.where(
                        lane < h,
                        pltpu.roll(low, (BR - j * h) % BR, 1),
                        jnp.where(
                            lane >= BR - h,
                            pltpu.roll(high, (2 * BR - h - j * h) % BR, 1),
                            jnp.zeros((C, BR), BF),
                        ),
                    )
                    v = jnp.concatenate([main[row], side], axis=1)
                    put_stack(ref, first + row, v, d, 2 * BR)
                return carry

            lax.fori_loop(0, packs, step, 0)

        nj = min(per, h)
        segment(self.top, 0, 0, per - nj, nj, h // nj)
        segment(self.own, h, e, 0, per, BC // per)
        segment(self.bottom, h + BC, e + BC // per, 0, nj, h // nj)


class Mirror:
    def __init__(self, place, refs):
        self.place = place
        self.out, self.land, self.send, self.recv, self.local = refs

    @staticmethod
    def scratch():
        return [
            pltpu.VMEM((8, BR, BR), BF),
            pltpu.VMEM((4, 8, BC, BR), BF),
            pltpu.SemaphoreType.DMA((4,)),
            pltpu.SemaphoreType.DMA((4,)),
            pltpu.SemaphoreType.DMA,
        ]

    def target(self, k):
        return self.place.ci // 4, 4 * self.place.ri + k

    def is_self(self, k):
        row, col = self.target(k)
        return (row == self.place.ri) & (col == self.place.ci)

    def copy(self, k, slot):
        return pltpu.make_async_remote_copy(
            src_ref=self.out.at[:, k * BC : k * BC + BC],
            dst_ref=self.land.at[slot],
            send_sem=self.send.at[k],
            recv_sem=self.recv.at[slot],
            device_id=self.target(k),
            device_id_type=MESH,
        )

    def keep(self, k):
        return pltpu.make_async_copy(
            self.out.at[:, k * BC : k * BC + BC],
            self.land.at[lax.rem(self.place.ci, 4)],
            self.local,
        )

    def start(self):
        slot = lax.rem(self.place.ci, 4)
        for k in range(4):

            @pl.when(self.is_self(k))
            def _():
                self.keep(k).start()

            @pl.when(jnp.logical_not(self.is_self(k)))
            def _():
                self.copy(k, slot).start()

    def wait(self):
        for k in range(4):

            @pl.when(self.is_self(k))
            def _():
                self.keep(k).wait()

            @pl.when(jnp.logical_not(self.is_self(k)))
            def _():
                self.copy(k, k).wait_recv()

    def drain(self):
        for k in range(4):

            @pl.when(jnp.logical_not(self.is_self(k)))
            def _():
                self.copy(k, k).wait_send()

    def fetch(self):
        lane = lax.broadcasted_iota(jnp.int32, (8, BC, BR), 2)
        half = lane < 64
        even = (lane // 32) % 2 == 0
        l0, l1, l2, l3 = (self.land[k] for k in range(4))
        a0 = jnp.where(half, l0, pltpu.roll(l2, 64, 2))
        a2 = jnp.where(half, pltpu.roll(l0, 64, 2), l2)
        a1 = jnp.where(half, l1, pltpu.roll(l3, 64, 2))
        a3 = jnp.where(half, pltpu.roll(l1, 64, 2), l3)
        return (
            jnp.where(even, a0, pltpu.roll(a1, 32, 2)),
            jnp.where(even, pltpu.roll(a0, 96, 2), a1),
            jnp.where(even, a2, pltpu.roll(a3, 32, 2)),
            jnp.where(even, pltpu.roll(a2, 96, 2), a3),
        )


class Place:
    def __init__(self, nrow, ncol):
        self.nrow = nrow
        self.ncol = ncol
        self.ri = lax.axis_index("row")
        self.ci = lax.axis_index("col")

    def inside(self, dr, dc):
        ok = None
        for index, step, size in ((self.ri, dr, self.nrow), (self.ci, dc, self.ncol)):
            if step:
                here = index < size - 1 if step > 0 else index > 0
                ok = here if ok is None else ok & here
        return ok


def interleave(groups):
    return jnp.concatenate(groups, axis=1)


def kernel_grad(padding, own, stacked, d, out, first):
    padding[...] = jnp.zeros(padding.shape, BF)

    def fill(k):
        padding[k + 2 * d] = own(k)

    rows(BC, fill)

    def step(t, acc):
        left = []
        right = []
        for u in range(8):
            k = t * 8 + u
            left.append(
                jnp.concatenate([padding[k + 2 * d], padding[k + d], padding[k]], axis=0)
            )
            right.append(stacked[k, :, 0:BR])
        return acc + lax.dot_general(
            jnp.concatenate(left, axis=1),
            jnp.concatenate(right, axis=1),
            (((1,), (1,)), ((), ())),
            preferred_element_type=F32,
        )

    total = lax.fori_loop(0, (BC + 2 * d) // 8, step, jnp.zeros((3 * C, 3 * C), F32))
    per = out.shape[1]
    for t in range(3 * C // per):
        out[first * (3 * C) // per + t, :, 0 : 3 * C] = total[t * per : t * per + per]


SCRATCH_COUNT = {"halo": 7, "mirror": 5}


def main_kernel(nrow, ncol, *refs):
    (x_ref, g_ref, fa, fb, sa, sb, dec, g0, kg) = refs[:9]
    rest = list(refs[9:])

    def take(n):
        out = rest[:n]
        del rest[:n]
        return out

    place = Place(nrow, ncol)
    ri, ci = place.ri, place.ci
    halo_x = Halo(8, place, take(7))
    halo_s2 = Halo(16, place, take(7))
    halo_z = Halo(16, place, take(7))
    halo_s1 = Halo(8, place, take(7))
    mir_g = Mirror(place, take(5))
    mir_y = Mirror(place, take(5))
    (wa1, wb1, wa2, wb2, wb2t, tb2, ta2, ta2t, tb1, ta1) = take(10)
    (xc1, hc1, slope1, xc2, sc2, hg2, hc2, hc2t, ec2, ec2t, sc1, ec1, y1, e2own, e1own) = take(15)
    (pad, acc, r1, mine, r2, fin, s1_send, s1_recv, s2_send, s2_recv, s3_send, s3_recv) = take(12)
    halos = (halo_x, halo_s2, halo_z, halo_s1)

    n1 = ncol // 2
    n2 = 2 * nrow
    a = lax.rem(ci, n1)
    half = ci // n1
    me2 = ri * 2 + half

    def group1(b):
        return ri, half * n1 + b

    def group2(m):
        return m // 2, lax.rem(m, 2) * n1 + a

    barrier = pltpu.get_barrier_semaphore()
    expected = jnp.int32(n1 + n2 - 2)

    def greet(row, col):
        pl.semaphore_signal(barrier, inc=1, device_id=(row, col), device_id_type=MESH)

    for dr in (-1, 0, 1):
        for dc in (-1, 0, 1):
            if dr or dc:
                ok = place.inside(dr, dc)
                expected = expected + ok.astype(jnp.int32)

                @pl.when(ok)
                def _():
                    greet(ri + dr, ci + dc)

    for k in range(4):
        away = jnp.logical_not(mir_g.is_self(k))
        expected = expected + away.astype(jnp.int32)

        @pl.when(away)
        def _():
            greet(*mir_g.target(k))

    def greet1(b, carry):
        @pl.when(b != a)
        def _():
            greet(*group1(b))

        return carry

    def greet2(m, carry):
        @pl.when(m != me2)
        def _():
            greet(*group2(m))

        return carry

    lax.fori_loop(0, n1, greet1, 0)
    lax.fori_loop(0, n2, greet2, 0)

    order = permutation(False)
    flat = x_ref[...].reshape(C * BC, BR)
    halo_x.own[...] = interleave(
        [dot(order, flat[256 * t : 256 * t + 256]).reshape(BC, 8, BR) for t in range(4)]
    ).astype(BF)
    gflat = g_ref[...].reshape(C * BC, BR)
    for j in range(8):
        mir_g.out[j] = gflat[j * BR : j * BR + BR].T
    for halo in halos:
        halo.fill_edges()
    pl.semaphore_wait(barrier, expected)
    halo_x.start()
    mir_g.start()

    fill_matrix(wa1, 0, fa, False, False)
    fill_matrix(wb1, 0, fb, False, False)
    fill_matrix(wa2, 0, sa, False, False)
    fill_matrix(wa2, C, sa, False, True)
    fill_matrix(wb2, 0, sb, False, False)
    fill_matrix(wb2t, 0, sb, False, True)
    fill_matrix(tb2, 0, sb, True, False)
    fill_matrix(tb2, C, sb, True, True)
    fill_matrix(ta2, 0, sa, True, False)
    fill_matrix(ta2t, 0, sa, True, True)
    fill_matrix(tb1, 0, fb, True, False)
    fill_matrix(ta1, 0, fa, True, False)

    lane = lax.broadcasted_iota(jnp.int32, (C, 2 * BR), 1)
    first_lane = jnp.where(ri < nrow - 1, BR, BR + 64)
    last_lane = jnp.where(ri > 0, 2 * BR, BR + 64)
    lane_ok = (lane < BR) | ((lane >= first_lane) & (lane < last_lane))

    def on_map(row, v):
        bin_index = ci * BC + row
        ok = (bin_index >= 0) & (bin_index < ncol * BC)
        return jnp.where(lane_ok & ok, v, 0.0)

    d = DILATE_ONE
    halo_x.wait()
    halo_x.build(xc1, d)

    def hidden1(k):
        pre = dot(wa1[...], taps(xc1, k, d))
        sig = jax.nn.sigmoid(pre)
        slope1[k] = sig * (1.0 + pre * (1.0 - sig))
        put_stack(hc1, k, on_map(k - d, pre * sig).astype(BF), d, BR)

    rows(BC + 2 * d, hidden1)

    def outer1(k):
        y1[k] = (halo_x.own[k].astype(F32) + dot(wb1[...], taps(hc1, k, d))).astype(BF)

    rows(BC, outer1)

    back = permutation(True)
    for t in range(4):
        part = y1[:, 8 * t : 8 * t + 8, :].reshape(256, BR)
        natural = dot(back, part)
        for j in range(2):
            mir_y.out[2 * t + j] = natural[j * BR : j * BR + BR].T.astype(BF)
    mir_y.start()

    mir_g.wait()
    turned = mir_g.fetch()
    parts = []
    for t in range(4):
        mirrored = jnp.concatenate(
            [turned[n][2 * t + j] for j in range(2) for n in range(4)], axis=0
        )
        here = gflat[256 * t : 256 * t + 256]
        mean = ((here.astype(F32) + mirrored.astype(F32)) * 0.5).astype(BF)
        parts.append(dot(order, mean).reshape(BC, 8, BR))
    halo_s2.own[...] = interleave(parts).astype(BF)
    halo_s2.start()

    mir_y.wait()
    turned = mir_y.fetch()
    parts = []
    for t in range(4):
        mirrored = jnp.concatenate(
            [turned[n][2 * t + j] for j in range(2) for n in range(4)], axis=0
        )
        parts.append(dot(order, mirrored).reshape(BC, 8, BR))
    halo_z.own[...] = ((y1[...].astype(F32) + interleave(parts)) * 0.5).astype(BF)
    halo_z.start()

    d = DILATE_TWO
    halo_s2.wait()
    halo_s2.build(sc2, d)

    def cotangent2(k):
        hg2[k] = dot(tb2[...], taps(sc2, k, d))

    rows(BC + 2 * d, cotangent2)
    halo_z.wait()
    halo_z.build(xc2, d)

    def hidden2(k):
        pre = dot(wa2[...], taps(xc2, k, d))
        sig = jax.nn.sigmoid(pre)
        hid = pre * sig
        grad = hg2[k] * (sig * (1.0 + pre * (1.0 - sig)))
        put_stack(hc2, k, on_map(k - d, hid[:C]).astype(BF), d, BR)
        put_stack(hc2t, k, on_map(k - d, hid[C:]).astype(BF), d, BR)
        put_stack(ec2, k, on_map(k - d, grad[:C]).astype(BF), d, BR)
        put_stack(ec2t, k, on_map(k - d, grad[C:]).astype(BF), d, BR)

    rows(BC + 2 * d, hidden2, 4)

    def upstream1(k):
        base = halo_s2.own[k].astype(F32)
        one = (base + dot(ta2[...], taps(ec2, k, d))).astype(BF)
        two = (base + dot(ta2t[...], taps(ec2t, k, d))).astype(BF)
        halo_s1.own[k] = ((one.astype(F32) + two.astype(F32)) * 0.5).astype(BF)

    rows(BC, upstream1)
    halo_s1.start()

    def outer2(k):
        base = halo_z.own[k].astype(F32)
        one = (base + dot(wb2[...], taps(hc2, k, d))).astype(BF)
        two = (base + dot(wb2t[...], taps(hc2t, k, d))).astype(BF)
        dec[k] = ((one.astype(F32) + two.astype(F32)) * 0.5).astype(BF)

    rows(BC, outer2)
    acc[...] = jnp.zeros(acc.shape, F32)
    kernel_grad(pad.at[0 : BC + 4 * d], lambda k: halo_s2.own[k], hc2, d, acc, 3)
    kernel_grad(
        pad.at[0 : BC + 4 * d], lambda k: ec2[k + DILATE_TWO, C : 2 * C, :], xc2.at[d : d + BC + 2 * d], d, acc, 2
    )

    d = DILATE_ONE
    kernel_grad(pad.at[0 : BC + 4 * d], lambda k: halo_s1.own[k], hc1, d, acc, 1)
    halo_s1.wait()
    halo_s1.build(sc1, d)

    def cotangent1(k):
        grad = dot(tb1[...], taps(sc1, k, d)) * slope1[k]
        put_stack(ec1, k, on_map(k - d, grad).astype(BF), d, BR)

    rows(BC + 2 * d, cotangent1)
    kernel_grad(
        pad.at[0 : BC + 4 * d], lambda k: ec1[k + DILATE_ONE, C : 2 * C, :], xc1.at[d : d + BC + 2 * d], d, acc, 0
    )

    def share(src, dst, send, recv, slot, device):
        return pltpu.make_async_remote_copy(
            src_ref=src, dst_ref=dst, send_sem=send, recv_sem=recv, device_id=device, device_id_type=MESH
        )

    def others(count, me, body):
        def step(b, carry):
            @pl.when(b != me)
            def _():
                body(b)

            return carry

        lax.fori_loop(0, count, step, 0)

    def scatter(b, slot):
        return share(acc.at[b], r1.at[slot], s1_send.at[b], s1_recv.at[slot], slot, group1(b))

    def spread(m, slot):
        return share(mine, r2.at[slot], s2_send.at[m], s2_recv.at[slot], slot, group2(m))

    def gather(b, slot):
        return share(fin.at[a], fin.at[slot], s3_send.at[b], s3_recv.at[slot], slot, group1(b))

    others(n1, a, lambda b: scatter(b, a).start())

    def upstream0(k):
        g0[k] = (halo_s1.own[k].astype(F32) + dot(ta1[...], taps(ec1, k, d))).astype(BF)

    rows(BC, upstream0)
    r1[a] = acc[a]
    others(n1, a, lambda b: scatter(b, b).wait_recv())
    mine[...] = lax.fori_loop(1, n1, lambda b, total: total + r1[b], r1[0])
    others(n2, me2, lambda m: spread(m, me2).start())
    r2[me2] = mine[...]
    others(n2, me2, lambda m: spread(m, m).wait_recv())
    fin[a] = lax.fori_loop(1, n2, lambda m, total: total + r2[m], r2[0])
    others(n1, a, lambda b: gather(b, a).start())
    for halo in halos:
        halo.drain()
    mir_g.drain()
    mir_y.drain()
    others(n1, a, lambda b: scatter(b, a).wait_send())
    others(n2, me2, lambda m: spread(m, me2).wait_send())
    others(n1, a, lambda b: gather(b, b).wait_recv())
    others(n1, a, lambda b: gather(b, a).wait_send())
    kg[...] = fin[...].reshape(kg.shape)


def finish_kernel(dec, g0, kg, out_dec, out_g0, out_a1, out_b1, out_a2, out_b2):
    back = permutation(True)
    for src, dst in ((dec, out_dec), (g0, out_g0)):
        whole = src[...].astype(F32)
        for t in range(4):
            part = whole[:, 8 * t : 8 * t + 8, :].reshape(256, BR).astype(BF)
            dst[8 * t : 8 * t + 8] = dot(back, part).astype(BF).reshape(8, BC, BR)
    for k, dst in enumerate((out_a1, out_b1, out_a2, out_b2)):
        for p in range(3):
            band = kg[(3 * k + p) * C : (3 * k + p) * C + C, :]
            for q in range(3):
                dst[p, q] = band[:, q * C : q * C + C]


def per_device(nrow, ncol, pair_map, out_grad, first_a, first_b, second_a, second_b):
    n1 = ncol // 2
    n2 = 2 * nrow
    per = 12 * C // n1
    wide = BC + 16
    vmem = pltpu.VMEM
    scratch = (
        Halo.scratch(8)
        + Halo.scratch(16)
        + Halo.scratch(16)
        + Halo.scratch(8)
        + Mirror.scratch()
        + Mirror.scratch()
        + [vmem((m, 9 * C), BF) for m in (C, C, 2 * C, C, C, 2 * C, C, C, C, C)]
        + [
            vmem((BC + 16, 3 * C, 2 * BR), BF),
            vmem((BC + 8, 3 * C, BR), BF),
            vmem((BC + 8, C, 2 * BR), F32),
            vmem((BC + 32, 3 * C, 2 * BR), BF),
            vmem((BC + 32, 3 * C, 2 * BR), BF),
            vmem((wide, 2 * C, 2 * BR), F32),
            vmem((wide, 3 * C, BR), BF),
            vmem((wide, 3 * C, BR), BF),
            vmem((wide, 3 * C, BR), BF),
            vmem((wide, 3 * C, BR), BF),
            vmem((BC + 16, 3 * C, 2 * BR), BF),
            vmem((BC + 8, 3 * C, BR), BF),
            vmem((BC, C, BR), BF),
            vmem((8, BR), F32),
            vmem((8, BR), F32),
        ]
        + [
            vmem((BC + 32, C, BR), BF),
            vmem((n1, per, BR), F32),
            vmem((n1, per, BR), F32),
            vmem((per, BR), F32),
            vmem((n2, per, BR), F32),
            vmem((n1, per, BR), F32),
        ]
        + [pltpu.SemaphoreType.DMA((n,)) for n in (n1, n1, n2, n2, n1, n1)]
    )
    whole = pl.BlockSpec(memory_space=pltpu.VMEM)
    dec, g0, kg = pl.pallas_call(
        functools.partial(main_kernel, nrow, ncol),
        out_shape=[
            jax.ShapeDtypeStruct((BC, C, BR), BF),
            jax.ShapeDtypeStruct((BC, C, BR), BF),
            jax.ShapeDtypeStruct((12 * C, BR), F32),
        ],
        in_specs=[whole] * 6,
        out_specs=[whole] * 3,
        scratch_shapes=scratch,
        compiler_params=pltpu.CompilerParams(
            collective_id=0, has_side_effects=True, vmem_limit_bytes=56 << 20
        ),
        name="blocks",
    )(pair_map, out_grad, first_a, first_b, second_a, second_b)
    small = jax.ShapeDtypeStruct((3, 3, C, C), F32)
    return pl.pallas_call(
        finish_kernel,
        out_shape=[
            jax.ShapeDtypeStruct((C, BC, BR), BF),
            jax.ShapeDtypeStruct((C, BC, BR), BF),
            small,
            small,
            small,
            small,
        ],
        in_specs=[whole] * 3,
        out_specs=[whole] * 6,
        compiler_params=pltpu.CompilerParams(vmem_limit_bytes=24 << 20),
        name="finish",
    )(dec, g0, kg)


def solution(mesh):
    return jax.shard_map(
        functools.partial(per_device, mesh.shape["row"], mesh.shape["col"]),
        mesh=mesh,
        in_specs=(P(None, "col", "row"), P(None, "col", "row"), P(), P(), P(), P()),
        out_specs=(P(None, "col", "row"), P(None, "col", "row"), P(), P(), P(), P()),
        check_vma=False,
    )
```

```python
import functools

import jax
import jax.numpy as jnp
from jax import lax
from jax.experimental import pallas as pl
from jax.experimental.pallas import tpu as pltpu
from jax.sharding import PartitionSpec as P

C = 32
BC = 32
BR = 128
DILATE_ONE = 4
DILATE_TWO = 8
MESH = pl.DeviceIdType.MESH
BF = jnp.bfloat16
F32 = jnp.float32


def dot(a, b):
    return jnp.dot(a, b, preferred_element_type=F32)


def permutation(inverse):
    row = lax.broadcasted_iota(jnp.int32, (256, 256), 0)
    col = lax.broadcasted_iota(jnp.int32, (256, 256), 1)
    if inverse:
        row, col = col, row
    same = (row // 8 == col % 32) & (row % 8 == col // 32)
    return jnp.where(same, 1.0, 0.0).astype(BF)


def fill_matrix(ref, row, kernel, flip, swap):
    for p in range(3):
        for q in range(3):
            a, b = (q, p) if swap else (p, q)
            if flip:
                piece = kernel[2 - a, 2 - b].astype(F32).T.astype(BF)
            else:
                piece = kernel[a, b]
            tap = 3 * p + q
            ref[row : row + C, tap * C : tap * C + C] = piece


def stack_shifts(v, d, lanes):
    return (
        pltpu.roll(v, d, 1)[:, :lanes],
        v[:, :lanes],
        pltpu.roll(v, 2 * BR - d, 1)[:, :lanes],
    )


def put_stack(ref, row, v, d, lanes):
    for q, part in enumerate(stack_shifts(v, d, lanes)):
        ref[row, q * C : q * C + C, :] = part


def taps(ref, row, d):
    return jnp.concatenate([ref[row], ref[row + d], ref[row + 2 * d]], axis=0)


def rows(count, body, unroll=8):
    def step(t, carry):
        for u in range(unroll):
            body(t * unroll + u)
        return carry

    lax.fori_loop(0, count // unroll, step, 0)


class Halo:
    names = ("own", "top", "bottom", "pack", "land", "send", "recv")

    def __init__(self, width, place, refs):
        self.h = width
        self.per = BR // width
        self.edge = 16 // self.per
        self.count = BC // self.per
        self.place = place
        self.own, self.top, self.bottom, self.pack, self.land, self.send, self.recv = refs

    @staticmethod
    def scratch(width):
        per = BR // width
        return [
            pltpu.VMEM((BC, C, BR), BF),
            pltpu.VMEM((width, C, BR), BF),
            pltpu.VMEM((width, C, BR), BF),
            pltpu.VMEM((2, BC // per, C, BR), BF),
            pltpu.VMEM((2, 64 // per, C, BR), BF),
            pltpu.SemaphoreType.DMA((8,)),
            pltpu.SemaphoreType.DMA((8,)),
        ]

    def pieces(self):
        e, n, h = self.edge, self.count, self.h
        return (
            (0, -1, self.own.at[0:h], self.bottom),
            (0, 1, self.own.at[BC - h : BC], self.top),
            (-1, 0, self.pack.at[0], self.land.at[0, e : e + n]),
            (1, 0, self.pack.at[1], self.land.at[1, e : e + n]),
            (-1, -1, self.pack.at[0, 0:e], self.land.at[0, e + n :]),
            (-1, 1, self.pack.at[0, n - e : n], self.land.at[0, 0:e]),
            (1, -1, self.pack.at[1, 0:e], self.land.at[1, e + n :]),
            (1, 1, self.pack.at[1, n - e : n], self.land.at[1, 0:e]),
        )

    def copy(self, k, piece):
        dr, dc, src, dst = piece
        return pltpu.make_async_remote_copy(
            src_ref=src,
            dst_ref=dst,
            send_sem=self.send.at[k],
            recv_sem=self.recv.at[k],
            device_id=(self.place.ri + dr, self.place.ci + dc),
            device_id_type=MESH,
        )

    def fill_edges(self):
        for dr, dc, src, dst in self.pieces():

            @pl.when(jnp.logical_not(self.place.inside(-dr, -dc)))
            def _():
                dst[...] = jnp.zeros(dst.shape, BF)

    def start(self):
        h, per = self.h, self.per
        group = lax.broadcasted_iota(jnp.int32, (C, BR), 1) // h

        def pack(t, carry):
            low = jnp.zeros((C, BR), BF)
            high = jnp.zeros((C, BR), BF)
            for j in range(per):
                v = self.own[t * per + j]
                low = jnp.where(group == j, pltpu.roll(v, j * h, 1), low)
                high = jnp.where(group == j, pltpu.roll(v, (j * h + h) % BR, 1), high)
            self.pack[0, t] = low
            self.pack[1, t] = high
            return carry

        lax.fori_loop(0, self.count, pack, 0)
        for k, piece in enumerate(self.pieces()):

            @pl.when(self.place.inside(piece[0], piece[1]))
            def _():
                self.copy(k, piece).start()

    def wait(self):
        for k, piece in enumerate(self.pieces()):

            @pl.when(self.place.inside(-piece[0], -piece[1]))
            def _():
                self.copy(k, piece).wait_recv()

    def drain(self):
        for k, piece in enumerate(self.pieces()):

            @pl.when(self.place.inside(piece[0], piece[1]))
            def _():
                self.copy(k, piece).wait_send()

    def build(self, ref, d):
        h, per, e = self.h, self.per, self.edge
        lane = lax.broadcasted_iota(jnp.int32, (C, BR), 1)

        def segment(main, first, pack, j0, nj, packs):
            def step(t, carry):
                low = self.land[0, pack + t]
                high = self.land[1, pack + t]
                for u in range(nj):
                    j = j0 + u
                    row = t * nj + u
                    side = jnp.where(
                        lane < h,
                        pltpu.roll(low, (BR - j * h) % BR, 1),
                        jnp.where(
                            lane >= BR - h,
                            pltpu.roll(high, (2 * BR - h - j * h) % BR, 1),
                            jnp.zeros((C, BR), BF),
                        ),
                    )
                    v = jnp.concatenate([main[row], side], axis=1)
                    put_stack(ref, first + row, v, d, 2 * BR)
                return carry

            lax.fori_loop(0, packs, step, 0)

        nj = min(per, h)
        segment(self.top, 0, 0, per - nj, nj, h // nj)
        segment(self.own, h, e, 0, per, BC // per)
        segment(self.bottom, h + BC, e + BC // per, 0, nj, h // nj)


class Mirror:
    def __init__(self, place, refs):
        self.place = place
        self.n = place.nrow
        self.per = 8 // place.nrow
        self.ri = place.ri
        self.cq = place.ci // 4
        self.s = lax.rem(place.ci, 4)
        self.out, self.relay, self.land, self.send1, self.recv1, self.send2, self.recv2 = refs

    @staticmethod
    def scratch(nrow):
        return [
            pltpu.VMEM((8, BR, BR), BF),
            pltpu.VMEM((nrow, 8 // nrow, BR, BR), BF),
            pltpu.VMEM((4, 8, BC, BR), BF),
            pltpu.SemaphoreType.DMA((nrow,)),
            pltpu.SemaphoreType.DMA((nrow,)),
            pltpu.SemaphoreType.DMA((nrow, 4)),
            pltpu.SemaphoreType.DMA((4, nrow)),
        ]

    def relay_of(self, ri, cq, s, q):
        return 2 * (q // 2) + lax.rem(ri, 2), 4 * (2 * (cq // 2) + lax.rem(q, 2)) + s

    def source(self, w):
        return 2 * (w // 2) + lax.rem(self.ri, 2), 2 * (self.cq // 2) + lax.rem(w, 2)

    def my_w(self):
        return 2 * (self.ri // 2) + lax.rem(self.cq, 2)

    def my_q(self):
        return 2 * (self.ri // 2) + lax.rem(self.cq, 2)

    def first(self, q, w):
        return self.out.at[pl.ds(q * self.per, self.per)], self.relay.at[w], self.recv1.at[w]

    def second(self, w, k, slot, q):
        r0 = pl.multiple_of(k * BC, BC)
        return (
            self.relay.at[w, :, pl.ds(r0, BC)],
            self.land.at[slot, pl.ds(q * self.per, self.per)],
            self.recv2.at[slot, q],
        )

    def target1(self, q):
        return self.relay_of(self.ri, self.cq, self.s, q)

    def target2(self, w, k):
        ri, cq = self.source(w)
        return cq, 4 * ri + k

    def is_self(self, device):
        return (device[0] == self.ri) & (device[1] == self.place.ci)

    def copy(self, parts, send, device):
        src, dst, recv = parts
        return pltpu.make_async_remote_copy(
            src_ref=src, dst_ref=dst, send_sem=send, recv_sem=recv, device_id=device, device_id_type=MESH
        )

    def go(self, parts, send, device):
        here = self.is_self(device)

        @pl.when(here)
        def _():
            pltpu.make_async_copy(*parts).start()

        @pl.when(jnp.logical_not(here))
        def _():
            self.copy(parts, send, device).start()

    def arrived(self, parts, send):
        self.copy(parts, send, (self.ri, self.place.ci)).wait_recv()

    def start(self):
        w = self.my_w()

        def step(q, carry):
            self.go(self.first(q, w), self.send1.at[q], self.target1(q))
            return carry

        lax.fori_loop(0, self.n, step, 0)

    def forward(self):
        mine = self.my_q()

        def step(w, carry):
            self.arrived(self.first(0, w), self.send1.at[0])
            for k in range(4):
                self.go(self.second(w, k, self.s, mine), self.send2.at[w, k], self.target2(w, k))
            return carry

        lax.fori_loop(0, self.n, step, 0)

    def wait(self):
        def step(q, carry):
            for k in range(4):
                self.arrived(self.second(0, 0, k, q), self.send2.at[0, 0])
            return carry

        lax.fori_loop(0, self.n, step, 0)

    def drain(self):
        def step(q, carry):
            @pl.when(jnp.logical_not(self.is_self(self.target1(q))))
            def _():
                self.copy(self.first(q, 0), self.send1.at[q], self.target1(q)).wait_send()

            for k in range(4):

                @pl.when(jnp.logical_not(self.is_self(self.target2(q, k))))
                def _():
                    self.copy(self.second(q, k, 0, 0), self.send2.at[q, k], self.target2(q, k)).wait_send()

            return carry

        lax.fori_loop(0, self.n, step, 0)

    def greet(self, greet):
        def step(q, count):
            ri, cq = self.source(q)
            source = ri, 4 * cq + self.s

            @pl.when(jnp.logical_not(self.is_self(source)))
            def _():
                greet(*source)

            count = count + jnp.logical_not(self.is_self(self.target1(q))).astype(jnp.int32)
            for k in range(4):
                relay = self.relay_of(self.cq, self.ri, k, q)

                @pl.when(jnp.logical_not(self.is_self(relay)))
                def _():
                    greet(*relay)

                away = jnp.logical_not(self.is_self(self.target2(q, k)))
                count = count + away.astype(jnp.int32)
            return count

        return lax.fori_loop(0, self.n, step, jnp.int32(0))

    def fetch(self):
        lane = lax.broadcasted_iota(jnp.int32, (8, BC, BR), 2)
        half = lane < 64
        even = (lane // 32) % 2 == 0
        l0, l1, l2, l3 = (self.land[k] for k in range(4))
        a0 = jnp.where(half, l0, pltpu.roll(l2, 64, 2))
        a2 = jnp.where(half, pltpu.roll(l0, 64, 2), l2)
        a1 = jnp.where(half, l1, pltpu.roll(l3, 64, 2))
        a3 = jnp.where(half, pltpu.roll(l1, 64, 2), l3)
        return (
            jnp.where(even, a0, pltpu.roll(a1, 32, 2)),
            jnp.where(even, pltpu.roll(a0, 96, 2), a1),
            jnp.where(even, a2, pltpu.roll(a3, 32, 2)),
            jnp.where(even, pltpu.roll(a2, 96, 2), a3),
        )


class Place:
    def __init__(self, nrow, ncol):
        self.nrow = nrow
        self.ncol = ncol
        self.ri = lax.axis_index("row")
        self.ci = lax.axis_index("col")

    def inside(self, dr, dc):
        ok = None
        for index, step, size in ((self.ri, dr, self.nrow), (self.ci, dc, self.ncol)):
            if step:
                here = index < size - 1 if step > 0 else index > 0
                ok = here if ok is None else ok & here
        return ok


def interleave(groups):
    return jnp.concatenate(groups, axis=1)


def kernel_grad(padding, own, stacked, d, out, first):
    padding[...] = jnp.zeros(padding.shape, BF)

    def fill(k):
        padding[k + 2 * d] = own(k)

    rows(BC, fill)

    def step(t, acc):
        left = []
        right = []
        for u in range(8):
            k = t * 8 + u
            left.append(
                jnp.concatenate([padding[k + 2 * d], padding[k + d], padding[k]], axis=0)
            )
            right.append(stacked[k, :, 0:BR])
        return acc + lax.dot_general(
            jnp.concatenate(left, axis=1),
            jnp.concatenate(right, axis=1),
            (((1,), (1,)), ((), ())),
            preferred_element_type=F32,
        )

    total = lax.fori_loop(0, (BC + 2 * d) // 8, step, jnp.zeros((3 * C, 3 * C), F32))
    per = out.shape[1]
    for t in range(3 * C // per):
        out[first * (3 * C) // per + t, :, 0 : 3 * C] = total[t * per : t * per + per]


def main_kernel(nrow, ncol, *refs):
    (x_ref, g_ref, fa, fb, sa, sb, dec, g0, kg) = refs[:9]
    rest = list(refs[9:])

    def take(n):
        out = rest[:n]
        del rest[:n]
        return out

    place = Place(nrow, ncol)
    ri, ci = place.ri, place.ci
    halo_x = Halo(8, place, take(7))
    halo_s2 = Halo(16, place, take(7))
    halo_z = Halo(16, place, take(7))
    halo_s1 = Halo(8, place, take(7))
    mir_g = Mirror(place, take(7))
    mir_y = Mirror(place, take(7))
    (wa1, wb1, wa2, wb2, wb2t, tb2, ta2, ta2t, tb1, ta1) = take(10)
    (xc1, hc1, slope1, xc2, sc2, hg2, hc2, hc2t, ec2, ec2t, sc1, ec1, y1, e2own, e1own) = take(15)
    (pad, acc, r1, mine, r2, fin, s1_send, s1_recv, s2_send, s2_recv, s3_send, s3_recv) = take(12)
    halos = (halo_x, halo_s2, halo_z, halo_s1)

    n1 = ncol // 2
    n2 = 2 * nrow
    a = lax.rem(ci, n1)
    half = ci // n1
    me2 = ri * 2 + half

    def group1(b):
        return ri, half * n1 + b

    def group2(m):
        return m // 2, lax.rem(m, 2) * n1 + a

    barrier = pltpu.get_barrier_semaphore()
    expected = jnp.int32(n1 + n2 - 2)

    def greet(row, col):
        pl.semaphore_signal(barrier, inc=1, device_id=(row, col), device_id_type=MESH)

    for dr in (-1, 0, 1):
        for dc in (-1, 0, 1):
            if dr or dc:
                ok = place.inside(dr, dc)
                expected = expected + ok.astype(jnp.int32)

                @pl.when(ok)
                def _():
                    greet(ri + dr, ci + dc)

    expected = expected + mir_g.greet(greet)

    def greet1(b, carry):
        @pl.when(b != a)
        def _():
            greet(*group1(b))

        return carry

    def greet2(m, carry):
        @pl.when(m != me2)
        def _():
            greet(*group2(m))

        return carry

    lax.fori_loop(0, n1, greet1, 0)
    lax.fori_loop(0, n2, greet2, 0)

    order = permutation(False)
    flat = x_ref[...].reshape(C * BC, BR)
    halo_x.own[...] = interleave(
        [dot(order, flat[256 * t : 256 * t + 256]).reshape(BC, 8, BR) for t in range(4)]
    ).astype(BF)
    gflat = g_ref[...].reshape(C * BC, BR)
    for j in range(8):
        mir_g.out[j] = gflat[j * BR : j * BR + BR].T
    for halo in halos:
        halo.fill_edges()
    pl.semaphore_wait(barrier, expected)
    halo_x.start()
    mir_g.start()

    fill_matrix(wa1, 0, fa, False, False)
    fill_matrix(wb1, 0, fb, False, False)
    fill_matrix(wa2, 0, sa, False, False)
    fill_matrix(wa2, C, sa, False, True)
    fill_matrix(wb2, 0, sb, False, False)
    fill_matrix(wb2t, 0, sb, False, True)
    fill_matrix(tb2, 0, sb, True, False)
    fill_matrix(tb2, C, sb, True, True)
    fill_matrix(ta2, 0, sa, True, False)
    fill_matrix(ta2t, 0, sa, True, True)
    fill_matrix(tb1, 0, fb, True, False)
    fill_matrix(ta1, 0, fa, True, False)

    lane = lax.broadcasted_iota(jnp.int32, (C, 2 * BR), 1)
    first_lane = jnp.where(ri < nrow - 1, BR, BR + 64)
    last_lane = jnp.where(ri > 0, 2 * BR, BR + 64)
    lane_ok = (lane < BR) | ((lane >= first_lane) & (lane < last_lane))

    def on_map(row, v):
        bin_index = ci * BC + row
        ok = (bin_index >= 0) & (bin_index < ncol * BC)
        return jnp.where(lane_ok & ok, v, 0.0)

    d = DILATE_ONE
    halo_x.wait()
    halo_x.build(xc1, d)

    def hidden1(k):
        pre = dot(wa1[...], taps(xc1, k, d))
        sig = jax.nn.sigmoid(pre)
        slope1[k] = sig * (1.0 + pre * (1.0 - sig))
        put_stack(hc1, k, on_map(k - d, pre * sig).astype(BF), d, BR)

    rows(BC + 2 * d, hidden1)
    mir_g.forward()

    def outer1(k):
        y1[k] = (halo_x.own[k].astype(F32) + dot(wb1[...], taps(hc1, k, d))).astype(BF)

    rows(BC, outer1)

    back = permutation(True)
    for t in range(4):
        part = y1[:, 8 * t : 8 * t + 8, :].reshape(256, BR)
        natural = dot(back, part)
        for j in range(2):
            mir_y.out[2 * t + j] = natural[j * BR : j * BR + BR].T.astype(BF)
    mir_y.start()

    mir_g.wait()
    turned = mir_g.fetch()
    parts = []
    for t in range(4):
        mirrored = jnp.concatenate(
            [turned[n][2 * t + j] for j in range(2) for n in range(4)], axis=0
        )
        here = gflat[256 * t : 256 * t + 256]
        mean = ((here.astype(F32) + mirrored.astype(F32)) * 0.5).astype(BF)
        parts.append(dot(order, mean).reshape(BC, 8, BR))
    halo_s2.own[...] = interleave(parts).astype(BF)
    halo_s2.start()
    mir_y.forward()

    mir_y.wait()
    turned = mir_y.fetch()
    parts = []
    for t in range(4):
        mirrored = jnp.concatenate(
            [turned[n][2 * t + j] for j in range(2) for n in range(4)], axis=0
        )
        parts.append(dot(order, mirrored).reshape(BC, 8, BR))
    halo_z.own[...] = ((y1[...].astype(F32) + interleave(parts)) * 0.5).astype(BF)
    halo_z.start()

    d = DILATE_TWO
    halo_s2.wait()
    halo_s2.build(sc2, d)

    def cotangent2(k):
        hg2[k] = dot(tb2[...], taps(sc2, k, d))

    rows(BC + 2 * d, cotangent2)
    halo_z.wait()
    halo_z.build(xc2, d)

    def hidden2(k):
        pre = dot(wa2[...], taps(xc2, k, d))
        sig = jax.nn.sigmoid(pre)
        hid = pre * sig
        grad = hg2[k] * (sig * (1.0 + pre * (1.0 - sig)))
        put_stack(hc2, k, on_map(k - d, hid[:C]).astype(BF), d, BR)
        put_stack(hc2t, k, on_map(k - d, hid[C:]).astype(BF), d, BR)
        put_stack(ec2, k, on_map(k - d, grad[:C]).astype(BF), d, BR)
        put_stack(ec2t, k, on_map(k - d, grad[C:]).astype(BF), d, BR)

    rows(BC + 2 * d, hidden2, 4)

    def upstream1(k):
        base = halo_s2.own[k].astype(F32)
        one = (base + dot(ta2[...], taps(ec2, k, d))).astype(BF)
        two = (base + dot(ta2t[...], taps(ec2t, k, d))).astype(BF)
        halo_s1.own[k] = ((one.astype(F32) + two.astype(F32)) * 0.5).astype(BF)

    rows(BC, upstream1)
    halo_s1.start()

    def outer2(k):
        base = halo_z.own[k].astype(F32)
        one = (base + dot(wb2[...], taps(hc2, k, d))).astype(BF)
        two = (base + dot(wb2t[...], taps(hc2t, k, d))).astype(BF)
        dec[k] = ((one.astype(F32) + two.astype(F32)) * 0.5).astype(BF)

    rows(BC, outer2)
    acc[...] = jnp.zeros(acc.shape, F32)
    kernel_grad(pad.at[0 : BC + 4 * d], lambda k: halo_s2.own[k], hc2, d, acc, 3)
    kernel_grad(
        pad.at[0 : BC + 4 * d], lambda k: ec2[k + DILATE_TWO, C : 2 * C, :], xc2.at[d : d + BC + 2 * d], d, acc, 2
    )

    d = DILATE_ONE
    kernel_grad(pad.at[0 : BC + 4 * d], lambda k: halo_s1.own[k], hc1, d, acc, 1)
    halo_s1.wait()
    halo_s1.build(sc1, d)

    def cotangent1(k):
        grad = dot(tb1[...], taps(sc1, k, d)) * slope1[k]
        put_stack(ec1, k, on_map(k - d, grad).astype(BF), d, BR)

    rows(BC + 2 * d, cotangent1)
    kernel_grad(
        pad.at[0 : BC + 4 * d], lambda k: ec1[k + DILATE_ONE, C : 2 * C, :], xc1.at[d : d + BC + 2 * d], d, acc, 0
    )

    def share(src, dst, send, recv, slot, device):
        return pltpu.make_async_remote_copy(
            src_ref=src, dst_ref=dst, send_sem=send, recv_sem=recv, device_id=device, device_id_type=MESH
        )

    def others(count, me, body):
        def step(b, carry):
            @pl.when(b != me)
            def _():
                body(b)

            return carry

        lax.fori_loop(0, count, step, 0)

    def scatter(b, slot):
        return share(acc.at[b], r1.at[slot], s1_send.at[b], s1_recv.at[slot], slot, group1(b))

    def spread(m, slot):
        return share(mine, r2.at[slot], s2_send.at[m], s2_recv.at[slot], slot, group2(m))

    def gather(b, slot):
        return share(fin.at[a], fin.at[slot], s3_send.at[b], s3_recv.at[slot], slot, group1(b))

    others(n1, a, lambda b: scatter(b, a).start())

    def upstream0(k):
        g0[k] = (halo_s1.own[k].astype(F32) + dot(ta1[...], taps(ec1, k, d))).astype(BF)

    rows(BC, upstream0)
    r1[a] = acc[a]
    others(n1, a, lambda b: scatter(b, b).wait_recv())
    mine[...] = lax.fori_loop(1, n1, lambda b, total: total + r1[b], r1[0])
    others(n2, me2, lambda m: spread(m, me2).start())
    r2[me2] = mine[...]
    others(n2, me2, lambda m: spread(m, m).wait_recv())
    fin[a] = lax.fori_loop(1, n2, lambda m, total: total + r2[m], r2[0])
    others(n1, a, lambda b: gather(b, a).start())
    for halo in halos:
        halo.drain()
    mir_g.drain()
    mir_y.drain()
    others(n1, a, lambda b: scatter(b, a).wait_send())
    others(n2, me2, lambda m: spread(m, me2).wait_send())
    others(n1, a, lambda b: gather(b, b).wait_recv())
    others(n1, a, lambda b: gather(b, a).wait_send())
    kg[...] = fin[...].reshape(kg.shape)


def finish_kernel(dec, g0, kg, out_dec, out_g0, out_a1, out_b1, out_a2, out_b2):
    back = permutation(True)
    for src, dst in ((dec, out_dec), (g0, out_g0)):
        whole = src[...].astype(F32)
        for t in range(4):
            part = whole[:, 8 * t : 8 * t + 8, :].reshape(256, BR).astype(BF)
            dst[8 * t : 8 * t + 8] = dot(back, part).astype(BF).reshape(8, BC, BR)
    for k, dst in enumerate((out_a1, out_b1, out_a2, out_b2)):
        for p in range(3):
            band = kg[(3 * k + p) * C : (3 * k + p) * C + C, :]
            for q in range(3):
                dst[p, q] = band[:, q * C : q * C + C]


def per_device(nrow, ncol, pair_map, out_grad, first_a, first_b, second_a, second_b):
    n1 = ncol // 2
    n2 = 2 * nrow
    per = 12 * C // n1
    wide = BC + 16
    vmem = pltpu.VMEM
    scratch = (
        Halo.scratch(8)
        + Halo.scratch(16)
        + Halo.scratch(16)
        + Halo.scratch(8)
        + Mirror.scratch(nrow)
        + Mirror.scratch(nrow)
        + [vmem((m, 9 * C), BF) for m in (C, C, 2 * C, C, C, 2 * C, C, C, C, C)]
        + [
            vmem((BC + 16, 3 * C, 2 * BR), BF),
            vmem((BC + 8, 3 * C, BR), BF),
            vmem((BC + 8, C, 2 * BR), F32),
            vmem((BC + 32, 3 * C, 2 * BR), BF),
            vmem((BC + 32, 3 * C, 2 * BR), BF),
            vmem((wide, 2 * C, 2 * BR), F32),
            vmem((wide, 3 * C, BR), BF),
            vmem((wide, 3 * C, BR), BF),
            vmem((wide, 3 * C, BR), BF),
            vmem((wide, 3 * C, BR), BF),
            vmem((BC + 16, 3 * C, 2 * BR), BF),
            vmem((BC + 8, 3 * C, BR), BF),
            vmem((BC, C, BR), BF),
            vmem((8, BR), F32),
            vmem((8, BR), F32),
        ]
        + [
            vmem((BC + 32, C, BR), BF),
            vmem((n1, per, BR), F32),
            vmem((n1, per, BR), F32),
            vmem((per, BR), F32),
            vmem((n2, per, BR), F32),
            vmem((n1, per, BR), F32),
        ]
        + [pltpu.SemaphoreType.DMA((n,)) for n in (n1, n1, n2, n2, n1, n1)]
    )
    whole = pl.BlockSpec(memory_space=pltpu.VMEM)
    dec, g0, kg = pl.pallas_call(
        functools.partial(main_kernel, nrow, ncol),
        out_shape=[
            jax.ShapeDtypeStruct((BC, C, BR), BF),
            jax.ShapeDtypeStruct((BC, C, BR), BF),
            jax.ShapeDtypeStruct((12 * C, BR), F32),
        ],
        in_specs=[whole] * 6,
        out_specs=[whole] * 3,
        scratch_shapes=scratch,
        compiler_params=pltpu.CompilerParams(
            collective_id=0, has_side_effects=True, vmem_limit_bytes=56 << 20
        ),
        name="blocks",
    )(pair_map, out_grad, first_a, first_b, second_a, second_b)
    small = jax.ShapeDtypeStruct((3, 3, C, C), F32)
    return pl.pallas_call(
        finish_kernel,
        out_shape=[
            jax.ShapeDtypeStruct((C, BC, BR), BF),
            jax.ShapeDtypeStruct((C, BC, BR), BF),
            small,
            small,
            small,
            small,
        ],
        in_specs=[whole] * 3,
        out_specs=[whole] * 6,
        compiler_params=pltpu.CompilerParams(vmem_limit_bytes=24 << 20),
        name="finish",
    )(dec, g0, kg)


def solution(mesh):
    return jax.shard_map(
        functools.partial(per_device, mesh.shape["row"], mesh.shape["col"]),
        mesh=mesh,
        in_specs=(P(None, "col", "row"), P(None, "col", "row"), P(), P(), P(), P()),
        out_specs=(P(None, "col", "row"), P(None, "col", "row"), P(), P(), P(), P()),
        check_vma=False,
    )
```

```python
import functools

import jax
import jax.numpy as jnp
from jax import lax
from jax.experimental import pallas as pl
from jax.experimental.pallas import tpu as pltpu
from jax.sharding import PartitionSpec as P

C = 32
BC = 32
BR = 128
DILATE_ONE = 4
DILATE_TWO = 8
MESH = pl.DeviceIdType.MESH
BF = jnp.bfloat16
F32 = jnp.float32


def dot(a, b):
    return jnp.dot(a, b, preferred_element_type=F32)


def permutation(inverse):
    row = lax.broadcasted_iota(jnp.int32, (256, 256), 0)
    col = lax.broadcasted_iota(jnp.int32, (256, 256), 1)
    if inverse:
        row, col = col, row
    same = (row // 8 == col % 32) & (row % 8 == col // 32)
    return jnp.where(same, 1.0, 0.0).astype(BF)


def fill_matrix(ref, row, kernel, flip, swap):
    for p in range(3):
        for q in range(3):
            a, b = (q, p) if swap else (p, q)
            if flip:
                piece = kernel[2 - a, 2 - b].astype(F32).T.astype(BF)
            else:
                piece = kernel[a, b]
            tap = 3 * p + q
            ref[row : row + C, tap * C : tap * C + C] = piece


def put_stack(ref, row, main, side, d, wide=False):
    lane = lax.broadcasted_iota(jnp.int32, (C, BR), 1)
    last = lane >= BR - d
    first = lane < d
    ref[row, 0:C, 0:BR] = pltpu.roll(jnp.where(last, side, main), d, 1)
    ref[row, C : 2 * C, 0:BR] = main
    ref[row, 2 * C : 3 * C, 0:BR] = pltpu.roll(jnp.where(first, side, main), BR - d, 1)
    if wide:
        ref[row, 0:C, BR : 2 * BR] = pltpu.roll(jnp.where(last, main, side), d, 1)
        ref[row, C : 2 * C, BR : 2 * BR] = side
        ref[row, 2 * C : 3 * C, BR : 2 * BR] = pltpu.roll(jnp.where(first, main, side), BR - d, 1)


def taps(ref, row, d):
    return jnp.concatenate([ref[row], ref[row + d], ref[row + 2 * d]], axis=0)


def rows(count, body, unroll=8):
    def step(t, carry):
        for u in range(unroll):
            body(t * unroll + u)
        return carry

    lax.fori_loop(0, count // unroll, step, 0)


class Halo:
    names = ("own", "top", "bottom", "pack", "land", "send", "recv")

    def __init__(self, width, place, refs):
        self.h = width
        self.per = BR // width
        self.edge = 16 // self.per
        self.count = BC // self.per
        self.place = place
        self.own, self.top, self.bottom, self.pack, self.land, self.send, self.recv = refs

    @staticmethod
    def scratch(width):
        per = BR // width
        return [
            pltpu.VMEM((BC, C, BR), BF),
            pltpu.VMEM((width, C, BR), BF),
            pltpu.VMEM((width, C, BR), BF),
            pltpu.VMEM((2, BC // per, C, BR), BF),
            pltpu.VMEM((2, 64 // per, C, BR), BF),
            pltpu.SemaphoreType.DMA((8,)),
            pltpu.SemaphoreType.DMA((8,)),
        ]

    def pieces(self):
        e, n, h = self.edge, self.count, self.h
        return (
            (0, -1, self.own.at[0:h], self.bottom),
            (0, 1, self.own.at[BC - h : BC], self.top),
            (-1, 0, self.pack.at[0], self.land.at[0, e : e + n]),
            (1, 0, self.pack.at[1], self.land.at[1, e : e + n]),
            (-1, -1, self.pack.at[0, 0:e], self.land.at[0, e + n :]),
            (-1, 1, self.pack.at[0, n - e : n], self.land.at[0, 0:e]),
            (1, -1, self.pack.at[1, 0:e], self.land.at[1, e + n :]),
            (1, 1, self.pack.at[1, n - e : n], self.land.at[1, 0:e]),
        )

    def copy(self, k, piece):
        dr, dc, src, dst = piece
        return pltpu.make_async_remote_copy(
            src_ref=src,
            dst_ref=dst,
            send_sem=self.send.at[k],
            recv_sem=self.recv.at[k],
            device_id=(self.place.ri + dr, self.place.ci + dc),
            device_id_type=MESH,
        )

    def fill_edges(self):
        for dr, dc, src, dst in self.pieces():

            @pl.when(jnp.logical_not(self.place.inside(-dr, -dc)))
            def _():
                dst[...] = jnp.zeros(dst.shape, BF)

    def pack_sides(self):
        h, per = self.h, self.per
        group = lax.broadcasted_iota(jnp.int32, (C, BR), 1) // h

        def pack(t, carry):
            low = jnp.zeros((C, BR), BF)
            high = jnp.zeros((C, BR), BF)
            for j in range(per):
                v = self.own[t * per + j]
                turned = pltpu.roll(v, j * h, 1) if j else v
                low = jnp.where(group == j, turned, low)
                high = jnp.where(group == (j - 1) % per, turned, high)
            self.pack[0, t] = low
            self.pack[1, t] = high
            return carry

        lax.fori_loop(0, self.count, pack, 0)

    def start(self):
        for k, piece in enumerate(self.pieces()):

            @pl.when(self.place.inside(piece[0], piece[1]))
            def _():
                self.copy(k, piece).start()

    def wait(self):
        for k, piece in enumerate(self.pieces()):

            @pl.when(self.place.inside(-piece[0], -piece[1]))
            def _():
                self.copy(k, piece).wait_recv()

    def drain(self):
        for k, piece in enumerate(self.pieces()):

            @pl.when(self.place.inside(piece[0], piece[1]))
            def _():
                self.copy(k, piece).wait_send()

    def build(self, ref, d):
        h, per, e = self.h, self.per, self.edge
        group = lax.broadcasted_iota(jnp.int32, (C, BR), 1) // h

        def segment(main, first, pack, j0, nj, packs):
            def step(t, carry):
                low = self.land[0, pack + t]
                high = self.land[1, pack + t]
                for u in range(nj):
                    j = j0 + u
                    row = t * nj + u
                    side = jnp.where(
                        group == j,
                        low,
                        jnp.where(group == (j - 1) % per, high, jnp.zeros((C, BR), BF)),
                    )
                    if j:
                        side = pltpu.roll(side, BR - j * h, 1)
                    put_stack(ref, first + row, main[row], side, d, True)
                return carry

            lax.fori_loop(0, packs, step, 0)

        nj = min(per, h)
        segment(self.top, 0, 0, per - nj, nj, h // nj)
        segment(self.own, h, e, 0, per, BC // per)
        segment(self.bottom, h + BC, e + BC // per, 0, nj, h // nj)


class Mirror:
    def __init__(self, place, refs):
        self.place = place
        self.n = place.nrow
        self.per = 8 // place.nrow
        self.ri = place.ri
        self.cq = place.ci // 4
        self.s = lax.rem(place.ci, 4)
        self.out, self.relay, self.land, self.send1, self.recv1, self.send2, self.recv2 = refs

    @staticmethod
    def scratch(nrow):
        return [
            pltpu.VMEM((8, BR, BR), BF),
            pltpu.VMEM((nrow, 8 // nrow, BR, BR), BF),
            pltpu.VMEM((4, 8, BC, BR), BF),
            pltpu.SemaphoreType.DMA((nrow,)),
            pltpu.SemaphoreType.DMA((nrow,)),
            pltpu.SemaphoreType.DMA((nrow, 4)),
            pltpu.SemaphoreType.DMA((4, nrow)),
        ]

    def relay_of(self, ri, cq, s, q):
        other = lax.rem(s + 2 * lax.rem(q + cq, 2), 4)
        return 2 * (q // 2) + lax.rem(ri, 2), 4 * (2 * (cq // 2) + lax.rem(q, 2)) + other

    def source(self, w):
        return (
            2 * (w // 2) + lax.rem(self.ri, 2),
            2 * (self.cq // 2) + lax.rem(w, 2),
            lax.rem(self.s + 2 * lax.rem(w + self.cq, 2), 4),
        )

    def my_w(self):
        return 2 * (self.ri // 2) + lax.rem(self.cq, 2)

    def my_q(self):
        return 2 * (self.ri // 2) + lax.rem(self.cq, 2)

    def first(self, q, w):
        return self.out.at[pl.ds(q * self.per, self.per)], self.relay.at[w], self.recv1.at[w]

    def second(self, w, k, slot, q):
        r0 = pl.multiple_of(k * BC, BC)
        return (
            self.relay.at[w, :, pl.ds(r0, BC)],
            self.land.at[slot, pl.ds(q * self.per, self.per)],
            self.recv2.at[slot, q],
        )

    def target1(self, q):
        return self.relay_of(self.ri, self.cq, self.s, q)

    def target2(self, w, k):
        ri, cq, _ = self.source(w)
        return cq, 4 * ri + k

    def is_self(self, device):
        return (device[0] == self.ri) & (device[1] == self.place.ci)

    def copy(self, parts, send, device):
        src, dst, recv = parts
        return pltpu.make_async_remote_copy(
            src_ref=src, dst_ref=dst, send_sem=send, recv_sem=recv, device_id=device, device_id_type=MESH
        )

    def go(self, parts, send, device):
        here = self.is_self(device)

        @pl.when(here)
        def _():
            pltpu.make_async_copy(*parts).start()

        @pl.when(jnp.logical_not(here))
        def _():
            self.copy(parts, send, device).start()

    def arrived(self, parts, send):
        self.copy(parts, send, (self.ri, self.place.ci)).wait_recv()

    def start(self):
        w = self.my_w()

        def step(q, carry):
            self.go(self.first(q, w), self.send1.at[q], self.target1(q))
            return carry

        lax.fori_loop(0, self.n, step, 0)

    def forward(self):
        mine = self.my_q()

        def step(w, carry):
            self.arrived(self.first(0, w), self.send1.at[0])
            slot = self.source(w)[2]
            for k in range(4):
                self.go(self.second(w, k, slot, mine), self.send2.at[w, k], self.target2(w, k))
            return carry

        lax.fori_loop(0, self.n, step, 0)

    def wait(self):
        def step(q, carry):
            for k in range(4):
                self.arrived(self.second(0, 0, k, q), self.send2.at[0, 0])
            return carry

        lax.fori_loop(0, self.n, step, 0)

    def drain(self):
        def step(q, carry):
            @pl.when(jnp.logical_not(self.is_self(self.target1(q))))
            def _():
                self.copy(self.first(q, 0), self.send1.at[q], self.target1(q)).wait_send()

            for k in range(4):

                @pl.when(jnp.logical_not(self.is_self(self.target2(q, k))))
                def _():
                    self.copy(self.second(q, k, 0, 0), self.send2.at[q, k], self.target2(q, k)).wait_send()

            return carry

        lax.fori_loop(0, self.n, step, 0)

    def greet(self, greet):
        def step(q, count):
            ri, cq, s = self.source(q)
            source = ri, 4 * cq + s

            @pl.when(jnp.logical_not(self.is_self(source)))
            def _():
                greet(*source)

            count = count + jnp.logical_not(self.is_self(self.target1(q))).astype(jnp.int32)
            for k in range(4):
                relay = self.relay_of(self.cq, self.ri, k, q)

                @pl.when(jnp.logical_not(self.is_self(relay)))
                def _():
                    greet(*relay)

                away = jnp.logical_not(self.is_self(self.target2(q, k)))
                count = count + away.astype(jnp.int32)
            return count

        return lax.fori_loop(0, self.n, step, jnp.int32(0))

    def fetch(self):
        lane = lax.broadcasted_iota(jnp.int32, (8, BC, BR), 2)
        half = lane < 64
        even = (lane // 32) % 2 == 0
        l0, l1, l2, l3 = (self.land[k] for k in range(4))
        a0 = jnp.where(half, l0, pltpu.roll(l2, 64, 2))
        a2 = jnp.where(half, pltpu.roll(l0, 64, 2), l2)
        a1 = jnp.where(half, l1, pltpu.roll(l3, 64, 2))
        a3 = jnp.where(half, pltpu.roll(l1, 64, 2), l3)
        return (
            jnp.where(even, a0, pltpu.roll(a1, 32, 2)),
            jnp.where(even, pltpu.roll(a0, 96, 2), a1),
            jnp.where(even, a2, pltpu.roll(a3, 32, 2)),
            jnp.where(even, pltpu.roll(a2, 96, 2), a3),
        )


class Place:
    def __init__(self, nrow, ncol):
        self.nrow = nrow
        self.ncol = ncol
        self.ri = lax.axis_index("row")
        self.ci = lax.axis_index("col")

    def inside(self, dr, dc):
        ok = None
        for index, step, size in ((self.ri, dr, self.nrow), (self.ci, dc, self.ncol)):
            if step:
                here = index < size - 1 if step > 0 else index > 0
                ok = here if ok is None else ok & here
        return ok


def interleave(groups):
    return jnp.concatenate(groups, axis=1)


class Total:
    def __init__(self, place, refs):
        self.place = place
        self.acc, self.r1, self.mine, self.r2, self.fin = refs[:5]
        self.send1, self.recv1, self.send2, self.recv2, self.send3, self.recv3 = refs[5:]
        self.owners = self.acc.shape[0]
        self.n1 = place.ncol // 2
        self.n2 = 2 * place.nrow
        self.a = lax.rem(place.ci, self.n1)
        self.half = place.ci // self.n1
        self.m = place.ri * 2 + self.half
        self.owner = self.a < self.owners

    @staticmethod
    def scratch(n1, n2, owners, count):
        block = (count, 3 * C // owners, BR)
        vmem = pltpu.VMEM
        return [
            vmem((owners,) + block, F32),
            vmem((n1,) + block, F32),
            vmem(block, F32),
            vmem((n2,) + block, F32),
            vmem((owners,) + block, F32),
        ] + [pltpu.SemaphoreType.DMA((n,)) for n in (owners, n1, n2, n2, n1, owners)]

    def group1(self, b):
        return self.place.ri, self.half * self.n1 + b

    def group2(self, m):
        return m // 2, lax.rem(m, 2) * self.n1 + self.a

    def others(self, count, me, body):
        def step(b, carry):
            @pl.when(b != me)
            def _():
                body(b)

            return carry

        lax.fori_loop(0, count, step, 0)

    def share(self, src, dst, send, recv, device):
        return pltpu.make_async_remote_copy(
            src_ref=src, dst_ref=dst, send_sem=send, recv_sem=recv, device_id=device, device_id_type=MESH
        )

    def scatter(self, b, slot):
        return self.share(
            self.acc.at[b], self.r1.at[slot], self.send1.at[b], self.recv1.at[slot], self.group1(b)
        )

    def spread(self, m, slot):
        return self.share(
            self.mine, self.r2.at[slot], self.send2.at[m], self.recv2.at[slot], self.group2(m)
        )

    def gather(self, b, src, slot):
        return self.share(
            self.fin.at[src], self.fin.at[slot], self.send3.at[b], self.recv3.at[slot], self.group1(b)
        )

    def start1(self):
        self.others(self.owners, self.a, lambda b: self.scatter(b, self.a).start())

    def start2(self):
        @pl.when(self.owner)
        def _():
            self.r1[self.a] = self.acc[self.a]
            self.others(self.n1, self.a, lambda b: self.scatter(0, b).wait_recv())
            self.mine[...] = sum(self.r1[b] for b in range(self.n1))
            self.others(self.n2, self.m, lambda m: self.spread(m, self.m).start())
            self.r2[self.m] = self.mine[...]

    def start3(self):
        @pl.when(self.owner)
        def _():
            self.others(self.n2, self.m, lambda m: self.spread(m, m).wait_recv())
            self.fin[self.a] = sum(self.r2[m] for m in range(self.n2))
            self.others(self.n1, self.a, lambda b: self.gather(b, self.a, self.a).start())

    def finish(self):
        self.others(self.owners, self.a, lambda b: self.gather(0, 0, b).wait_recv())

    def drain(self):
        self.others(self.owners, self.a, lambda b: self.scatter(b, 0).wait_send())

        @pl.when(self.owner)
        def _():
            self.others(self.n2, self.m, lambda m: self.spread(m, 0).wait_send())
            self.others(self.n1, self.a, lambda b: self.gather(b, self.a, 0).wait_send())


def kernel_grad(padding, own, stacked, d, out, which):
    def fill(k):
        padding[k + 2 * d] = own(k)

    rows(BC, fill, 16)
    total = jnp.zeros((3 * C, 3 * C), F32)
    for t in range((BC + 2 * d) // 8):
        left = []
        right = []
        for k in range(t * 8, t * 8 + 8):
            left.append(
                jnp.concatenate([padding[k + 2 * d], padding[k + d], padding[k]], axis=0)
            )
            right.append(stacked[k, :, 0:BR])
        total = total + lax.dot_general(
            jnp.concatenate(left, axis=1),
            jnp.concatenate(right, axis=1),
            (((1,), (1,)), ((), ())),
            preferred_element_type=F32,
        )
    per = out.shape[2]
    for t in range(3 * C // per):
        out[t, which, :, 0 : 3 * C] = total[t * per : t * per + per]


def main_kernel(nrow, ncol, *refs):
    inputs, (dec_out, g0_out, early_out, late_out) = refs[:6], refs[6:10]
    rest = list(refs[10:])

    def take(n):
        out = rest[:n]
        del rest[:n]
        return out

    place = Place(nrow, ncol)
    ri, ci = place.ri, place.ci
    halo_x = Halo(8, place, take(7))
    halo_s2 = Halo(16, place, take(7))
    halo_z = Halo(16, place, take(7))
    halo_s1 = Halo(8, place, take(7))
    halos = (halo_x, halo_s2, halo_z, halo_s1)
    mir_g = Mirror(place, take(7))
    mir_y = Mirror(place, take(7))
    early = Total(place, take(11))
    late = Total(place, take(11))
    held = take(6)
    x_ref, g_ref, fa, fb, sa, sb = held
    in_sem, out_sem = take(2)
    (wa1, wb1, wa2, wb2, wb2t, tb2, ta2, ta2t, tb1, ta1) = take(10)
    (xc1, hc1, slope1, xc2, sc2, hg2, hc2, hc2t, ec2, ec2t, sc1, ec1, y1, dec, g0) = take(15)
    pad1, pad2 = take(2)

    loads = [
        pltpu.make_async_copy(src, dst, in_sem.at[k]) for k, (src, dst) in enumerate(zip(inputs, held))
    ]
    for load in loads:
        load.start()

    barrier = pltpu.get_barrier_semaphore()
    expected = jnp.int32(early.n1 + early.n2 - 2)

    def greet(row, col):
        pl.semaphore_signal(barrier, inc=1, device_id=(row, col), device_id_type=MESH)

    for dr in (-1, 0, 1):
        for dc in (-1, 0, 1):
            if dr or dc:
                ok = place.inside(dr, dc)
                expected = expected + ok.astype(jnp.int32)

                @pl.when(ok)
                def _():
                    greet(ri + dr, ci + dc)

    expected = expected + mir_g.greet(greet)
    early.others(early.n1, early.a, lambda b: greet(*early.group1(b)))
    early.others(early.n2, early.m, lambda m: greet(*early.group2(m)))

    order = permutation(False)
    loads[0].wait()
    flat = x_ref[...].reshape(C * BC, BR)
    halo_x.own[...] = interleave(
        [dot(order, flat[256 * t : 256 * t + 256]).reshape(BC, 8, BR) for t in range(4)]
    ).astype(BF)
    halo_x.pack_sides()
    for load in loads[1:]:
        load.wait()
    gflat = g_ref[...].reshape(C * BC, BR)
    for j in range(8):
        mir_g.out[j] = gflat[j * BR : j * BR + BR].T
    fill_matrix(wa1, 0, fa, False, False)
    fill_matrix(wb1, 0, fb, False, False)
    pl.semaphore_wait(barrier, expected)
    halo_x.start()
    mir_g.start()

    fill_matrix(wa2, 0, sa, False, False)
    fill_matrix(wa2, C, sa, False, True)
    fill_matrix(wb2, 0, sb, False, False)
    fill_matrix(wb2t, 0, sb, False, True)
    fill_matrix(tb2, 0, sb, True, False)
    fill_matrix(tb2, C, sb, True, True)
    fill_matrix(ta2, 0, sa, True, False)
    fill_matrix(ta2t, 0, sa, True, True)
    fill_matrix(tb1, 0, fb, True, False)
    fill_matrix(ta1, 0, fa, True, False)
    for halo in halos:
        halo.fill_edges()
    for ref in (pad1, pad2, early.acc, late.acc):
        ref[...] = jnp.zeros(ref.shape, ref.dtype)

    lane = lax.broadcasted_iota(jnp.int32, (C, BR), 1)
    first_lane = jnp.where(ri < nrow - 1, 0, 64)
    last_lane = jnp.where(ri > 0, BR, 64)
    side_ok = (lane >= first_lane) & (lane < last_lane)

    def put_field(ref, k, d, v):
        bin_index = ci * BC + k - d
        ok = (bin_index >= 0) & (bin_index < ncol * BC)
        main = jnp.where(ok, v[:, :BR], 0.0).astype(BF)
        side = jnp.where(side_ok & ok, v[:, BR:], 0.0).astype(BF)
        put_stack(ref, k, main, side, d)

    d = DILATE_ONE
    halo_x.wait()
    halo_x.build(xc1, d)

    def hidden1(k):
        pre = dot(wa1[...], taps(xc1, k, d))
        sig = jax.nn.sigmoid(pre)
        slope1[k] = sig * (1.0 + pre * (1.0 - sig))
        put_field(hc1, k, d, pre * sig)

    rows(BC + 2 * d, hidden1, 10)
    mir_g.forward()

    def outer1(k):
        y1[k] = (halo_x.own[k].astype(F32) + dot(wb1[...], taps(hc1, k, d))).astype(BF)

    rows(BC, outer1, 16)

    back = permutation(True)
    for t in range(4):
        part = y1[:, 8 * t : 8 * t + 8, :].reshape(256, BR)
        natural = dot(back, part)
        for j in range(2):
            mir_y.out[2 * t + j] = natural[j * BR : j * BR + BR].T.astype(BF)
    mir_y.start()

    mir_g.wait()
    turned = mir_g.fetch()
    parts = []
    for t in range(4):
        mirrored = jnp.concatenate(
            [turned[n][2 * t + j] for j in range(2) for n in range(4)], axis=0
        )
        here = gflat[256 * t : 256 * t + 256]
        mean = ((here.astype(F32) + mirrored.astype(F32)) * 0.5).astype(BF)
        parts.append(dot(order, mean).reshape(BC, 8, BR))
    halo_s2.own[...] = interleave(parts).astype(BF)
    halo_s2.pack_sides()
    halo_s2.start()
    mir_y.forward()
    halo_s2.wait()
    halo_s2.build(sc2, DILATE_TWO)

    mir_y.wait()
    turned = mir_y.fetch()
    parts = []
    for t in range(4):
        mirrored = jnp.concatenate(
            [turned[n][2 * t + j] for j in range(2) for n in range(4)], axis=0
        )
        parts.append(dot(order, mirrored).reshape(BC, 8, BR))
    halo_z.own[...] = ((y1[...].astype(F32) + interleave(parts)) * 0.5).astype(BF)
    halo_z.pack_sides()
    halo_z.start()

    d = DILATE_TWO

    def cotangent2(k):
        hg2[k] = dot(tb2[...], taps(sc2, k, d))

    rows(BC + 2 * d, cotangent2, 16)
    halo_z.wait()
    halo_z.build(xc2, d)

    def hidden2(k):
        pre = dot(wa2[...], taps(xc2, k, d))
        sig = jax.nn.sigmoid(pre)
        hid = pre * sig
        grad = hg2[k] * (sig * (1.0 + pre * (1.0 - sig)))
        put_field(hc2, k, d, hid[:C])
        put_field(hc2t, k, d, hid[C:])
        put_field(ec2, k, d, grad[:C])
        put_field(ec2t, k, d, grad[C:])

    rows(BC + 2 * d, hidden2, 8)

    def upstream1(k):
        base = halo_s2.own[k].astype(F32)
        one = (base + dot(ta2[...], taps(ec2, k, d))).astype(BF)
        two = (base + dot(ta2t[...], taps(ec2t, k, d))).astype(BF)
        halo_s1.own[k] = ((one.astype(F32) + two.astype(F32)) * 0.5).astype(BF)

    rows(BC, upstream1, 16)
    halo_s1.pack_sides()
    halo_s1.start()
    kernel_grad(pad2, lambda k: halo_s2.own[k], hc2, d, early.acc, 2)
    kernel_grad(
        pad2, lambda k: ec2[k + DILATE_TWO, C : 2 * C, :], xc2.at[d : d + BC + 2 * d], d, early.acc, 1
    )

    d = DILATE_ONE
    kernel_grad(pad1, lambda k: halo_s1.own[k], hc1, d, early.acc, 0)
    early.start1()
    halo_s1.wait()
    halo_s1.build(sc1, d)

    def cotangent1(k):
        put_field(ec1, k, d, dot(tb1[...], taps(sc1, k, d)) * slope1[k])

    rows(BC + 2 * d, cotangent1, 10)
    kernel_grad(
        pad1, lambda k: ec1[k + DILATE_ONE, C : 2 * C, :], xc1.at[d : d + BC + 2 * d], d, late.acc, 0
    )
    late.start1()
    early.start2()

    def upstream0(k):
        g0[k] = (halo_s1.own[k].astype(F32) + dot(ta1[...], taps(ec1, k, d))).astype(BF)

    rows(BC, upstream0, 16)
    g0_copy = pltpu.make_async_copy(g0, g0_out, out_sem.at[0])
    g0_copy.start()
    late.start2()

    def outer2(k):
        base = halo_z.own[k].astype(F32)
        one = (base + dot(wb2[...], taps(hc2, k, DILATE_TWO))).astype(BF)
        two = (base + dot(wb2t[...], taps(hc2t, k, DILATE_TWO))).astype(BF)
        dec[k] = ((one.astype(F32) + two.astype(F32)) * 0.5).astype(BF)

    rows(BC, outer2, 16)
    dec_copy = pltpu.make_async_copy(dec, dec_out, out_sem.at[1])
    dec_copy.start()
    early.start3()
    late.start3()
    for halo in halos:
        halo.drain()
    mir_g.drain()
    mir_y.drain()
    early.finish()
    early_copy = pltpu.make_async_copy(early.fin, early_out, out_sem.at[2])
    early_copy.start()
    late.finish()
    late_copy = pltpu.make_async_copy(late.fin, late_out, out_sem.at[3])
    late_copy.start()
    early.drain()
    late.drain()
    for copy in (g0_copy, dec_copy, early_copy, late_copy):
        copy.wait()


def finish_kernel(dec_in, g0_in, early_in, late_in, out_dec, out_g0, out_a1, out_b1, out_a2, out_b2, *rest):
    held, sems = rest[:4], rest[4]
    loads = [
        pltpu.make_async_copy(src, dst, sems.at[k])
        for k, (src, dst) in enumerate(zip((dec_in, g0_in, early_in, late_in), held))
    ]
    for load in loads:
        load.start()
    back = permutation(True)
    for load, src, dst in zip(loads, held, (out_dec, out_g0)):
        load.wait()
        whole = src[...].astype(F32)
        for t in range(4):
            part = whole[:, 8 * t : 8 * t + 8, :].reshape(256, BR).astype(BF)
            dst[8 * t : 8 * t + 8] = dot(back, part).astype(BF).reshape(8, BC, BR)
    early, late = held[2:]
    loads[2].wait()
    loads[3].wait()
    owners = early.shape[0]
    for src, which, dst in ((late, 0, out_a1), (early, 0, out_b1), (early, 1, out_a2), (early, 2, out_b2)):
        band = src[:, which].reshape(3 * C, BR)
        for p in range(3):
            for q in range(3):
                dst[p, q] = band[p * C : p * C + C, q * C : q * C + C]


def per_device(nrow, ncol, *arrays):
    n1 = ncol // 2
    n2 = 2 * nrow
    owners = 12 if n1 >= 12 else 4
    wide = BC + 16
    vmem = pltpu.VMEM
    grad_shapes = [(owners, count, 3 * C // owners, BR) for count in (3, 1)]
    scratch = (
        Halo.scratch(8)
        + Halo.scratch(16)
        + Halo.scratch(16)
        + Halo.scratch(8)
        + Mirror.scratch(nrow)
        + Mirror.scratch(nrow)
        + Total.scratch(n1, n2, owners, 3)
        + Total.scratch(n1, n2, owners, 1)
        + [vmem((C, BC, BR), BF)] * 2
        + [vmem((3, 3, C, C), BF)] * 4
        + [pltpu.SemaphoreType.DMA((6,)), pltpu.SemaphoreType.DMA((4,))]
        + [vmem((m, 9 * C), BF) for m in (C, C, 2 * C, C, C, 2 * C, C, C, C, C)]
        + [
            vmem((BC + 16, 3 * C, 2 * BR), BF),
            vmem((BC + 8, 3 * C, BR), BF),
            vmem((BC + 8, C, 2 * BR), F32),
            vmem((BC + 32, 3 * C, 2 * BR), BF),
            vmem((BC + 32, 3 * C, 2 * BR), BF),
            vmem((wide, 2 * C, 2 * BR), F32),
            vmem((wide, 3 * C, BR), BF),
            vmem((wide, 3 * C, BR), BF),
            vmem((wide, 3 * C, BR), BF),
            vmem((wide, 3 * C, BR), BF),
            vmem((BC + 16, 3 * C, 2 * BR), BF),
            vmem((BC + 8, 3 * C, BR), BF),
            vmem((BC, C, BR), BF),
            vmem((BC, C, BR), BF),
            vmem((BC, C, BR), BF),
            vmem((BC + 16, C, BR), BF),
            vmem((BC + 32, C, BR), BF),
        ]
    )
    whole = pl.BlockSpec(memory_space=pltpu.VMEM)
    anywhere = pl.BlockSpec(memory_space=pl.ANY)
    by_bin = jax.ShapeDtypeStruct((BC, C, BR), BF)
    results = pl.pallas_call(
        functools.partial(main_kernel, nrow, ncol),
        out_shape=[by_bin, by_bin] + [jax.ShapeDtypeStruct(shape, F32) for shape in grad_shapes],
        in_specs=[anywhere] * 6,
        out_specs=[anywhere] * 4,
        scratch_shapes=scratch,
        compiler_params=pltpu.CompilerParams(
            collective_id=0, has_side_effects=True, vmem_limit_bytes=56 << 20
        ),
        name="blocks",
    )(*arrays)
    small = jax.ShapeDtypeStruct((3, 3, C, C), F32)
    field = jax.ShapeDtypeStruct((C, BC, BR), BF)
    return pl.pallas_call(
        finish_kernel,
        out_shape=[field, field, small, small, small, small],
        in_specs=[anywhere] * 4,
        out_specs=[whole] * 6,
        scratch_shapes=[vmem((BC, C, BR), BF)] * 2
        + [vmem(shape, F32) for shape in grad_shapes]
        + [pltpu.SemaphoreType.DMA((4,))],
        compiler_params=pltpu.CompilerParams(vmem_limit_bytes=56 << 20),
        name="finish",
    )(*results)


def solution(mesh):
    return jax.shard_map(
        functools.partial(per_device, mesh.shape["row"], mesh.shape["col"]),
        mesh=mesh,
        in_specs=(P(None, "col", "row"), P(None, "col", "row"), P(), P(), P(), P()),
        out_specs=(P(None, "col", "row"), P(None, "col", "row"), P(), P(), P(), P()),
        check_vma=False,
    )
```

```python
import functools

import jax
import jax.numpy as jnp
from jax import lax
from jax.experimental import pallas as pl
from jax.experimental.pallas import tpu as pltpu
from jax.sharding import PartitionSpec as P

C = 32
BC = 32
BR = 128
DILATE_ONE = 4
DILATE_TWO = 8
MESH = pl.DeviceIdType.MESH
BF = jnp.bfloat16
F32 = jnp.float32


def dot(a, b):
    return jnp.dot(a, b, preferred_element_type=F32)


def permutation(inverse):
    row = lax.broadcasted_iota(jnp.int32, (256, 256), 0)
    col = lax.broadcasted_iota(jnp.int32, (256, 256), 1)
    if inverse:
        row, col = col, row
    same = (row // 8 == col % 32) & (row % 8 == col // 32)
    return jnp.where(same, 1.0, 0.0).astype(BF)


def fill_matrix(ref, row, kernel, flip, swap):
    for p in range(3):
        for q in range(3):
            a, b = (q, p) if swap else (p, q)
            if flip:
                piece = kernel[2 - a, 2 - b].astype(F32).T.astype(BF)
            else:
                piece = kernel[a, b]
            tap = 3 * p + q
            ref[row : row + C, tap * C : tap * C + C] = piece


def put_stack(ref, row, main, side, d, wide=False):
    lane = lax.broadcasted_iota(jnp.int32, (C, BR), 1)
    last = lane >= BR - d
    first = lane < d
    ref[row, 0:C, 0:BR] = pltpu.roll(jnp.where(last, side, main), d, 1)
    ref[row, C : 2 * C, 0:BR] = main
    ref[row, 2 * C : 3 * C, 0:BR] = pltpu.roll(jnp.where(first, side, main), BR - d, 1)
    if wide:
        ref[row, 0:C, BR : 2 * BR] = pltpu.roll(jnp.where(last, main, side), d, 1)
        ref[row, C : 2 * C, BR : 2 * BR] = side
        ref[row, 2 * C : 3 * C, BR : 2 * BR] = pltpu.roll(jnp.where(first, main, side), BR - d, 1)


def taps(ref, row, d):
    return jnp.concatenate([ref[row], ref[row + d], ref[row + 2 * d]], axis=0)


def rows(count, body, unroll=8, first=0):
    def step(t, carry):
        for u in range(unroll):
            body(first + t * unroll + u)
        return carry

    lax.fori_loop(0, count // unroll, step, 0)


def outer_rows(body, unroll):
    per = 16 // unroll

    def step(t, carry):
        for u in range(unroll):
            body(t * unroll + (t // per) * 16 + u)
        return carry

    lax.fori_loop(0, 2 * per, step, 0)


class Halo:
    names = ("own", "top", "bottom", "pack", "land", "send", "recv")

    def __init__(self, width, place, refs, by_way=False):
        self.h = width
        self.by_way = by_way
        self.per = BR // width
        self.edge = 16 // self.per
        self.count = BC // self.per
        self.place = place
        self.own, self.top, self.bottom, self.pack, self.land, self.send, self.recv = refs

    @staticmethod
    def scratch(width):
        per = BR // width
        return [
            pltpu.VMEM((BC, C, BR), BF),
            pltpu.VMEM((width, C, BR), BF),
            pltpu.VMEM((width, C, BR), BF),
            pltpu.VMEM((2, BC // per, C, BR), BF),
            pltpu.VMEM((2, 64 // per, C, BR), BF),
            pltpu.SemaphoreType.DMA((8,)),
            pltpu.SemaphoreType.DMA((8,)),
        ]

    def pieces(self):
        e, n, h = self.edge, self.count, self.h
        out = []
        for dr, dc, src, dst in (
            (0, -1, self.own.at[0:h], self.bottom),
            (0, 1, self.own.at[BC - h : BC], self.top),
            (-1, 0, self.pack.at[0], self.land.at[0, e : e + n]),
            (1, 0, self.pack.at[1], self.land.at[1, e : e + n]),
            (-1, -1, self.pack.at[0, 0:e], self.land.at[0, e + n :]),
            (-1, 1, self.pack.at[0, n - e : n], self.land.at[0, 0:e]),
            (1, -1, self.pack.at[1, 0:e], self.land.at[1, e + n :]),
            (1, 1, self.pack.at[1, n - e : n], self.land.at[1, 0:e]),
        ):
            target = (self.place.ri + dr, self.place.ci + dc)
            sends = self.place.inside(dr, dc)
            if self.by_way and dr and dc:
                side = 0 if dr < 0 else 1
                src = self.land.at[side, e : 2 * e] if dc < 0 else self.land.at[side, n : e + n]
                target = (self.place.ri, self.place.ci + dc)
                sends = self.place.inside(-dr, dc)
            out.append((dr, dc, src, dst, target, sends))
        return out

    def copy(self, k, piece):
        return pltpu.make_async_remote_copy(
            src_ref=piece[2],
            dst_ref=piece[3],
            send_sem=self.send.at[k],
            recv_sem=self.recv.at[k],
            device_id=piece[4],
            device_id_type=MESH,
        )

    def launch(self, which):
        for k, piece in enumerate(self.pieces()):
            if k in which:

                @pl.when(piece[5])
                def _():
                    self.copy(k, piece).start()

    def accept(self, which):
        for k, piece in enumerate(self.pieces()):
            if k in which:

                @pl.when(self.place.inside(-piece[0], -piece[1]))
                def _():
                    self.copy(k, piece).wait_recv()

    def start(self):
        self.launch((2, 3, 0, 1) if self.by_way else range(8))

    def forward(self):
        self.accept((2, 3))
        self.launch((4, 5, 6, 7))

    def wait(self):
        self.accept((0, 1, 4, 5, 6, 7) if self.by_way else range(8))

    def drain(self):
        for k, piece in enumerate(self.pieces()):

            @pl.when(piece[5])
            def _():
                self.copy(k, piece).wait_send()

    def fill_edges(self):
        for dr, dc, _, dst, _, _ in self.pieces():

            @pl.when(jnp.logical_not(self.place.inside(-dr, -dc)))
            def _():
                dst[...] = jnp.zeros(dst.shape, BF)

    def pack_sides(self):
        h, per = self.h, self.per
        group = lax.broadcasted_iota(jnp.int32, (C, BR), 1) // h

        def pack(t, carry):
            low = jnp.zeros((C, BR), BF)
            high = jnp.zeros((C, BR), BF)
            for j in range(per):
                v = self.own[t * per + j]
                turned = pltpu.roll(v, j * h, 1) if j else v
                low = jnp.where(group == j, turned, low)
                high = jnp.where(group == (j - 1) % per, turned, high)
            self.pack[0, t] = low
            self.pack[1, t] = high
            return carry

        lax.fori_loop(0, self.count, pack, 0)

    def prepare(self, ref, d):
        def own(k):
            main = self.own[k]
            ref[self.h + k, 0:C, 0:BR] = pltpu.roll(main, d, 1)
            ref[self.h + k, C : 2 * C, 0:BR] = main
            ref[self.h + k, 2 * C : 3 * C, 0:BR] = pltpu.roll(main, BR - d, 1)

        rows(BC, own, 16)

    def build(self, ref, d, inner=True, outer=True):
        h, per, e = self.h, self.per, self.edge
        lane = lax.broadcasted_iota(jnp.int32, (C, BR), 1)
        group = lane // h

        def complete(row, side):
            ref[row, C : 2 * C, BR : 2 * BR] = side
            for q, shift, edge in ((0, d, lane < d), (2, BR - d, lane >= BR - d)):
                there = ref[row, q * C : q * C + C, 0:BR]
                turned = pltpu.roll(side, shift, 1)
                ref[row, q * C : q * C + C, 0:BR] = jnp.where(edge, turned, there)
                ref[row, q * C : q * C + C, BR : 2 * BR] = jnp.where(edge, there, turned)

        def segment(main, first, pack, j0, nj, packs):
            def step(t, carry):
                low = self.land[0, pack + t]
                high = self.land[1, pack + t]
                for u in range(nj):
                    j = j0 + u
                    row = t * nj + u
                    side = jnp.where(
                        group == j,
                        low,
                        jnp.where(group == (j - 1) % per, high, jnp.zeros((C, BR), BF)),
                    )
                    if j:
                        side = pltpu.roll(side, BR - j * h, 1)
                    if main is self.own:
                        complete(first + row, side)
                    else:
                        put_stack(ref, first + row, main[row], side, d, True)
                return carry

            lax.fori_loop(0, packs, step, 0)

        nj = min(per, h)
        if inner:
            segment(self.own, h, e, 0, per, BC // per)
        if outer:
            segment(self.top, 0, 0, per - nj, nj, h // nj)
            segment(self.bottom, h + BC, e + BC // per, 0, nj, h // nj)


class Mirror:
    def __init__(self, place, refs):
        self.place = place
        self.n = place.nrow
        self.per = 8 // place.nrow
        self.ri = place.ri
        self.cq = place.ci // 4
        self.s = lax.rem(place.ci, 4)
        self.out, self.relay, self.land, self.send1, self.recv1, self.send2, self.recv2 = refs

    @staticmethod
    def scratch(nrow):
        return [
            pltpu.VMEM((8, BR, BR), BF),
            pltpu.VMEM((nrow, 8 // nrow, BR, BR), BF),
            pltpu.VMEM((4, 8, BC, BR), BF),
            pltpu.SemaphoreType.DMA((nrow,)),
            pltpu.SemaphoreType.DMA((nrow,)),
            pltpu.SemaphoreType.DMA((nrow, 4)),
            pltpu.SemaphoreType.DMA((4, nrow)),
        ]

    def relay_of(self, ri, cq, s, q):
        other = lax.rem(s + 2 * lax.rem(q + cq, 2), 4)
        return 2 * (q // 2) + lax.rem(ri, 2), 4 * (2 * (cq // 2) + lax.rem(q, 2)) + other

    def source(self, w):
        return (
            2 * (w // 2) + lax.rem(self.ri, 2),
            2 * (self.cq // 2) + lax.rem(w, 2),
            lax.rem(self.s + 2 * lax.rem(w + self.cq, 2), 4),
        )

    def my_w(self):
        return 2 * (self.ri // 2) + lax.rem(self.cq, 2)

    def my_q(self):
        return 2 * (self.ri // 2) + lax.rem(self.cq, 2)

    def first(self, q, w):
        return self.out.at[pl.ds(q * self.per, self.per)], self.relay.at[w], self.recv1.at[w]

    def second(self, w, k, slot, q):
        r0 = pl.multiple_of(k * BC, BC)
        return (
            self.relay.at[w, :, pl.ds(r0, BC)],
            self.land.at[slot, pl.ds(q * self.per, self.per)],
            self.recv2.at[slot, q],
        )

    def target1(self, q):
        return self.relay_of(self.ri, self.cq, self.s, q)

    def target2(self, w, k):
        ri, cq, _ = self.source(w)
        return cq, 4 * ri + k

    def is_self(self, device):
        return (device[0] == self.ri) & (device[1] == self.place.ci)

    def copy(self, parts, send, device):
        src, dst, recv = parts
        return pltpu.make_async_remote_copy(
            src_ref=src, dst_ref=dst, send_sem=send, recv_sem=recv, device_id=device, device_id_type=MESH
        )

    def go(self, parts, send, device):
        here = self.is_self(device)

        @pl.when(here)
        def _():
            pltpu.make_async_copy(*parts).start()

        @pl.when(jnp.logical_not(here))
        def _():
            self.copy(parts, send, device).start()

    def arrived(self, parts, send):
        self.copy(parts, send, (self.ri, self.place.ci)).wait_recv()

    def start(self):
        w = self.my_w()

        def step(q, carry):
            self.go(self.first(q, w), self.send1.at[q], self.target1(q))
            return carry

        lax.fori_loop(0, self.n, step, 0)

    def forward(self):
        mine = self.my_q()

        def step(w, carry):
            self.arrived(self.first(0, w), self.send1.at[0])
            slot = self.source(w)[2]
            for k in range(4):
                self.go(self.second(w, k, slot, mine), self.send2.at[w, k], self.target2(w, k))
            return carry

        lax.fori_loop(0, self.n, step, 0)

    def wait(self):
        def step(q, carry):
            for k in range(4):
                self.arrived(self.second(0, 0, k, q), self.send2.at[0, 0])
            return carry

        lax.fori_loop(0, self.n, step, 0)

    def drain(self):
        def step(q, carry):
            @pl.when(jnp.logical_not(self.is_self(self.target1(q))))
            def _():
                self.copy(self.first(q, 0), self.send1.at[q], self.target1(q)).wait_send()

            for k in range(4):

                @pl.when(jnp.logical_not(self.is_self(self.target2(q, k))))
                def _():
                    self.copy(self.second(q, k, 0, 0), self.send2.at[q, k], self.target2(q, k)).wait_send()

            return carry

        lax.fori_loop(0, self.n, step, 0)

    def greet(self, greet):
        def step(q, count):
            ri, cq, s = self.source(q)
            source = ri, 4 * cq + s

            @pl.when(jnp.logical_not(self.is_self(source)))
            def _():
                greet(*source)

            count = count + jnp.logical_not(self.is_self(self.target1(q))).astype(jnp.int32)
            for k in range(4):
                relay = self.relay_of(self.cq, self.ri, k, q)

                @pl.when(jnp.logical_not(self.is_self(relay)))
                def _():
                    greet(*relay)

                away = jnp.logical_not(self.is_self(self.target2(q, k)))
                count = count + away.astype(jnp.int32)
            return count

        return lax.fori_loop(0, self.n, step, jnp.int32(0))

    def fetch(self):
        lane = lax.broadcasted_iota(jnp.int32, (8, BC, BR), 2)
        half = lane < 64
        even = (lane // 32) % 2 == 0
        l0, l1, l2, l3 = (self.land[k] for k in range(4))
        a0 = jnp.where(half, l0, pltpu.roll(l2, 64, 2))
        a2 = jnp.where(half, pltpu.roll(l0, 64, 2), l2)
        a1 = jnp.where(half, l1, pltpu.roll(l3, 64, 2))
        a3 = jnp.where(half, pltpu.roll(l1, 64, 2), l3)
        return (
            jnp.where(even, a0, pltpu.roll(a1, 32, 2)),
            jnp.where(even, pltpu.roll(a0, 96, 2), a1),
            jnp.where(even, a2, pltpu.roll(a3, 32, 2)),
            jnp.where(even, pltpu.roll(a2, 96, 2), a3),
        )


class Place:
    def __init__(self, nrow, ncol):
        self.nrow = nrow
        self.ncol = ncol
        self.ri = lax.axis_index("row")
        self.ci = lax.axis_index("col")

    def inside(self, dr, dc):
        ok = None
        for index, step, size in ((self.ri, dr, self.nrow), (self.ci, dc, self.ncol)):
            if step:
                here = index < size - 1 if step > 0 else index > 0
                ok = here if ok is None else ok & here
        return ok


def interleave(groups):
    return jnp.concatenate(groups, axis=1)


class Total:
    def __init__(self, place, refs):
        self.place = place
        self.acc, self.r1, self.mine, self.r2, self.fin = refs[:5]
        self.send1, self.recv1, self.send2, self.recv2, self.send3, self.recv3 = refs[5:]
        self.owners = self.acc.shape[0]
        self.n1 = place.ncol // 2
        self.n2 = 2 * place.nrow
        self.a = lax.rem(place.ci, self.n1)
        self.half = place.ci // self.n1
        self.m = place.ri * 2 + self.half
        self.owner = self.a < self.owners

    @staticmethod
    def scratch(n1, n2, owners, count):
        block = (count, 3 * C // owners, BR)
        vmem = pltpu.VMEM
        return [
            vmem((owners,) + block, F32),
            vmem((n1,) + block, F32),
            vmem(block, F32),
            vmem((n2,) + block, F32),
            vmem((owners,) + block, F32),
        ] + [pltpu.SemaphoreType.DMA((n,)) for n in (owners, n1, n2, n2, n1, owners)]

    def group1(self, b):
        return self.place.ri, self.half * self.n1 + b

    def group2(self, m):
        return m // 2, lax.rem(m, 2) * self.n1 + self.a

    def others(self, count, me, body):
        def step(b, carry):
            @pl.when(b != me)
            def _():
                body(b)

            return carry

        lax.fori_loop(0, count, step, 0)

    def share(self, src, dst, send, recv, device):
        return pltpu.make_async_remote_copy(
            src_ref=src, dst_ref=dst, send_sem=send, recv_sem=recv, device_id=device, device_id_type=MESH
        )

    def scatter(self, b, slot):
        return self.share(
            self.acc.at[b], self.r1.at[slot], self.send1.at[b], self.recv1.at[slot], self.group1(b)
        )

    def spread(self, m, slot):
        return self.share(
            self.mine, self.r2.at[slot], self.send2.at[m], self.recv2.at[slot], self.group2(m)
        )

    def gather(self, b, src, slot):
        return self.share(
            self.fin.at[src], self.fin.at[slot], self.send3.at[b], self.recv3.at[slot], self.group1(b)
        )

    def start1(self):
        self.others(self.owners, self.a, lambda b: self.scatter(b, self.a).start())

    def start2(self):
        @pl.when(self.owner)
        def _():
            self.r1[self.a] = self.acc[self.a]
            self.others(self.n1, self.a, lambda b: self.scatter(0, b).wait_recv())
            self.mine[...] = sum(self.r1[b] for b in range(self.n1))
            self.others(self.n2, self.m, lambda m: self.spread(m, self.m).start())
            self.r2[self.m] = self.mine[...]

    def start3(self):
        @pl.when(self.owner)
        def _():
            self.others(self.n2, self.m, lambda m: self.spread(m, m).wait_recv())
            self.fin[self.a] = sum(self.r2[m] for m in range(self.n2))
            self.others(self.n1, self.a, lambda b: self.gather(b, self.a, self.a).start())

    def finish(self):
        self.others(self.owners, self.a, lambda b: self.gather(0, 0, b).wait_recv())

    def drain(self):
        self.others(self.owners, self.a, lambda b: self.scatter(b, 0).wait_send())

        @pl.when(self.owner)
        def _():
            self.others(self.n2, self.m, lambda m: self.spread(m, 0).wait_send())
            self.others(self.n1, self.a, lambda b: self.gather(b, self.a, 0).wait_send())


def kernel_grad(padding, own, stacked, d, out, which):
    def fill(k):
        padding[k + 2 * d] = own(k)

    rows(BC, fill, 16)
    total = jnp.zeros((3 * C, 3 * C), F32)
    for t in range((BC + 2 * d) // 8):
        left = []
        right = []
        for k in range(t * 8, t * 8 + 8):
            left.append(
                jnp.concatenate([padding[k + 2 * d], padding[k + d], padding[k]], axis=0)
            )
            right.append(stacked[k, :, 0:BR])
        total = total + lax.dot_general(
            jnp.concatenate(left, axis=1),
            jnp.concatenate(right, axis=1),
            (((1,), (1,)), ((), ())),
            preferred_element_type=F32,
        )
    per = out.shape[2]
    for t in range(3 * C // per):
        out[t, which, :, 0 : 3 * C] = total[t * per : t * per + per]


def main_kernel(nrow, ncol, *refs):
    inputs, (dec_out, g0_out, early_out, late_out) = refs[:6], refs[6:10]
    rest = list(refs[10:])

    def take(n):
        out = rest[:n]
        del rest[:n]
        return out

    place = Place(nrow, ncol)
    ri, ci = place.ri, place.ci
    halo_x = Halo(8, place, take(7))
    halo_s2 = Halo(16, place, take(7), True)
    halo_z = Halo(16, place, take(7), True)
    halo_s1 = Halo(8, place, take(7))
    halos = (halo_x, halo_s2, halo_z, halo_s1)
    mir_g = Mirror(place, take(7))
    mir_y = Mirror(place, take(7))
    early = Total(place, take(11))
    late = Total(place, take(11))
    held = take(6)
    x_ref, g_ref, fa, fb, sa, sb = held
    in_sem, out_sem = take(2)
    (wa1, wb1, wa2, wb2, wb2t, tb2, ta2, ta2t, tb1, ta1) = take(10)
    (xc1, hc1, slope1, xc2, sc2, hg2, hc2, hc2t, ec2, ec2t, sc1, ec1, y1, dec, g0) = take(15)
    pad1, pad2, dec_nat, g0_nat = take(4)

    loads = [
        pltpu.make_async_copy(src, dst, in_sem.at[k]) for k, (src, dst) in enumerate(zip(inputs, held))
    ]
    for load in loads:
        load.start()

    barrier = pltpu.get_barrier_semaphore()
    expected = jnp.int32(early.n1 + early.n2 - 2)

    def greet(row, col):
        pl.semaphore_signal(barrier, inc=1, device_id=(row, col), device_id_type=MESH)

    for dr in (-1, 0, 1):
        for dc in (-1, 0, 1):
            if dr or dc:
                ok = place.inside(dr, dc)
                expected = expected + ok.astype(jnp.int32)

                @pl.when(ok)
                def _():
                    greet(ri + dr, ci + dc)

    expected = expected + mir_g.greet(greet)
    early.others(early.n1, early.a, lambda b: greet(*early.group1(b)))
    early.others(early.n2, early.m, lambda m: greet(*early.group2(m)))

    order = permutation(False)
    loads[0].wait()
    flat = x_ref[...].reshape(C * BC, BR)
    halo_x.own[...] = interleave(
        [dot(order, flat[256 * t : 256 * t + 256]).reshape(BC, 8, BR) for t in range(4)]
    ).astype(BF)
    halo_x.pack_sides()
    for load in loads[1:]:
        load.wait()
    gflat = g_ref[...].reshape(C * BC, BR)
    for j in range(8):
        mir_g.out[j] = gflat[j * BR : j * BR + BR].T
    fill_matrix(wa1, 0, fa, False, False)
    fill_matrix(wb1, 0, fb, False, False)
    pl.semaphore_wait(barrier, expected)
    halo_x.start()
    mir_g.start()

    fill_matrix(wa2, 0, sa, False, False)
    fill_matrix(wa2, C, sa, False, True)
    fill_matrix(wb2, 0, sb, False, False)
    fill_matrix(wb2t, 0, sb, False, True)
    fill_matrix(tb2, 0, sb, True, False)
    fill_matrix(tb2, C, sb, True, True)
    fill_matrix(ta2, 0, sa, True, False)
    fill_matrix(ta2t, 0, sa, True, True)
    fill_matrix(tb1, 0, fb, True, False)
    fill_matrix(ta1, 0, fa, True, False)
    for halo in halos:
        halo.fill_edges()
    for ref in (pad1, pad2, early.acc, late.acc):
        ref[...] = jnp.zeros(ref.shape, ref.dtype)

    lane = lax.broadcasted_iota(jnp.int32, (C, BR), 1)
    first_lane = jnp.where(ri < nrow - 1, 0, 64)
    last_lane = jnp.where(ri > 0, BR, 64)
    side_ok = (lane >= first_lane) & (lane < last_lane)

    def put_field(ref, k, d, v):
        bin_index = ci * BC + k - d
        ok = (bin_index >= 0) & (bin_index < ncol * BC)
        main = jnp.where(ok, v[:, :BR], 0.0).astype(BF)
        side = jnp.where(side_ok & ok, v[:, BR:], 0.0).astype(BF)
        put_stack(ref, k, main, side, d)

    d = DILATE_ONE
    halo_x.prepare(xc1, d)
    halo_x.wait()
    mir_g.forward()
    halo_x.build(xc1, d)

    def hidden1(k):
        pre = dot(wa1[...], taps(xc1, k, d))
        sig = jax.nn.sigmoid(pre)
        slope1[k] = sig * (1.0 + pre * (1.0 - sig))
        put_field(hc1, k, d, pre * sig)

    rows(BC + 2 * d, hidden1, 10)

    def outer1(k):
        y1[k] = (halo_x.own[k].astype(F32) + dot(wb1[...], taps(hc1, k, d))).astype(BF)

    rows(BC, outer1, 16)

    back = permutation(True)
    for t in range(4):
        part = y1[:, 8 * t : 8 * t + 8, :].reshape(256, BR)
        natural = dot(back, part)
        for j in range(2):
            mir_y.out[2 * t + j] = natural[j * BR : j * BR + BR].T.astype(BF)
    mir_y.start()
    mir_y.forward()

    mir_g.wait()
    turned = mir_g.fetch()
    parts = []
    for t in range(4):
        mirrored = jnp.concatenate(
            [turned[n][2 * t + j] for j in range(2) for n in range(4)], axis=0
        )
        here = gflat[256 * t : 256 * t + 256]
        mean = ((here.astype(F32) + mirrored.astype(F32)) * 0.5).astype(BF)
        parts.append(dot(order, mean).reshape(BC, 8, BR))
    halo_s2.own[...] = interleave(parts).astype(BF)
    halo_s2.pack_sides()
    halo_s2.start()
    halo_s2.prepare(sc2, DILATE_TWO)
    halo_s2.forward()
    halo_s2.build(sc2, DILATE_TWO, outer=False)

    mir_y.wait()
    turned = mir_y.fetch()
    parts = []
    for t in range(4):
        mirrored = jnp.concatenate(
            [turned[n][2 * t + j] for j in range(2) for n in range(4)], axis=0
        )
        parts.append(dot(order, mirrored).reshape(BC, 8, BR))
    halo_z.own[...] = ((y1[...].astype(F32) + interleave(parts)) * 0.5).astype(BF)
    halo_z.pack_sides()
    halo_z.start()
    halo_z.prepare(xc2, DILATE_TWO)

    d = DILATE_TWO

    def cotangent2(k):
        hg2[k] = dot(tb2[...], taps(sc2, k, d))

    halo_s2.wait()
    halo_s2.build(sc2, d, inner=False)
    rows(BC + 2 * d, cotangent2, 16)
    halo_z.forward()
    halo_z.build(xc2, d, outer=False)

    def hidden2(k):
        pre = dot(wa2[...], taps(xc2, k, d))
        sig = jax.nn.sigmoid(pre)
        hid = pre * sig
        grad = hg2[k] * (sig * (1.0 + pre * (1.0 - sig)))
        hg2[k] = hid
        put_field(ec2, k, d, grad[:C])
        put_field(ec2t, k, d, grad[C:])

    rows(16, hidden2, 8, 16)
    halo_z.wait()
    halo_z.build(xc2, d, inner=False)
    outer_rows(hidden2, 8)

    def upstream1(k):
        base = halo_s2.own[k].astype(F32)
        one = (base + dot(ta2[...], taps(ec2, k, d))).astype(BF)
        two = (base + dot(ta2t[...], taps(ec2t, k, d))).astype(BF)
        halo_s1.own[k] = ((one.astype(F32) + two.astype(F32)) * 0.5).astype(BF)

    rows(BC, upstream1, 16)
    halo_s1.pack_sides()
    halo_s1.start()
    halo_s1.prepare(sc1, DILATE_ONE)

    def place2(k):
        put_field(hc2, k, DILATE_TWO, hg2[k, :C, :])

    rows(BC + 2 * d, place2)
    kernel_grad(pad2, lambda k: halo_s2.own[k], hc2, d, early.acc, 2)
    kernel_grad(
        pad2, lambda k: ec2[k + DILATE_TWO, C : 2 * C, :], xc2.at[d : d + BC + 2 * d], d, early.acc, 1
    )

    d = DILATE_ONE
    kernel_grad(pad1, lambda k: halo_s1.own[k], hc1, d, early.acc, 0)
    early.start1()
    halo_s1.wait()
    halo_s1.build(sc1, d)

    def cotangent1(k):
        put_field(ec1, k, d, dot(tb1[...], taps(sc1, k, d)) * slope1[k])

    rows(BC + 2 * d, cotangent1, 10)
    kernel_grad(
        pad1, lambda k: ec1[k + DILATE_ONE, C : 2 * C, :], xc1.at[d : d + BC + 2 * d], d, late.acc, 0
    )
    late.start1()
    early.start2()

    def by_channel(src, dst):
        for t in range(4):
            part = src[:, 8 * t : 8 * t + 8, :].reshape(256, BR)
            dst[8 * t : 8 * t + 8] = dot(back, part).astype(BF).reshape(8, BC, BR)

    def upstream0(k):
        g0[k] = (halo_s1.own[k].astype(F32) + dot(ta1[...], taps(ec1, k, d))).astype(BF)

    rows(BC, upstream0, 16)
    by_channel(g0, g0_nat)
    g0_copy = pltpu.make_async_copy(g0_nat, g0_out, out_sem.at[0])
    g0_copy.start()
    late.start2()

    def place2t(k):
        put_field(hc2t, k, DILATE_TWO, hg2[k, C:, :])

    rows(BC + 16, place2t)

    def outer2(k):
        base = halo_z.own[k].astype(F32)
        one = (base + dot(wb2[...], taps(hc2, k, DILATE_TWO))).astype(BF)
        two = (base + dot(wb2t[...], taps(hc2t, k, DILATE_TWO))).astype(BF)
        dec[k] = ((one.astype(F32) + two.astype(F32)) * 0.5).astype(BF)

    rows(BC, outer2, 16)
    by_channel(dec, dec_nat)
    dec_copy = pltpu.make_async_copy(dec_nat, dec_out, out_sem.at[1])
    dec_copy.start()
    early.start3()
    late.start3()
    for halo in halos:
        halo.drain()
    mir_g.drain()
    mir_y.drain()
    early.finish()
    early_copy = pltpu.make_async_copy(early.fin, early_out, out_sem.at[2])
    early_copy.start()
    late.finish()
    late_copy = pltpu.make_async_copy(late.fin, late_out, out_sem.at[3])
    late_copy.start()
    early.drain()
    late.drain()
    for copy in (g0_copy, dec_copy, early_copy, late_copy):
        copy.wait()


def finish_kernel(dec_in, g0_in, early_in, late_in, out_dec, out_g0, out_a1, out_b1, out_a2, out_b2, early, late, sems):
    copies = [
        pltpu.make_async_copy(src, dst, sems.at[k])
        for k, (src, dst) in enumerate(
            ((late_in, late), (early_in, early), (dec_in, out_dec), (g0_in, out_g0))
        )
    ]
    for copy in copies:
        copy.start()
    copies[0].wait()
    copies[1].wait()
    owners = early.shape[0]
    for src, which, dst in ((late, 0, out_a1), (early, 0, out_b1), (early, 1, out_a2), (early, 2, out_b2)):
        band = src[:, which].reshape(3 * C, BR)
        for p in range(3):
            for q in range(3):
                dst[p, q] = band[p * C : p * C + C, q * C : q * C + C]
    copies[2].wait()
    copies[3].wait()


def per_device(nrow, ncol, *arrays):
    n1 = ncol // 2
    n2 = 2 * nrow
    owners = 12 if n1 >= 12 else 4
    wide = BC + 16
    vmem = pltpu.VMEM
    grad_shapes = [(owners, count, 3 * C // owners, BR) for count in (3, 1)]
    scratch = (
        Halo.scratch(8)
        + Halo.scratch(16)
        + Halo.scratch(16)
        + Halo.scratch(8)
        + Mirror.scratch(nrow)
        + Mirror.scratch(nrow)
        + Total.scratch(n1, n2, owners, 3)
        + Total.scratch(n1, n2, owners, 1)
        + [vmem((C, BC, BR), BF)] * 2
        + [vmem((3, 3, C, C), BF)] * 4
        + [pltpu.SemaphoreType.DMA((6,)), pltpu.SemaphoreType.DMA((4,))]
        + [vmem((m, 9 * C), BF) for m in (C, C, 2 * C, C, C, 2 * C, C, C, C, C)]
        + [
            vmem((BC + 16, 3 * C, 2 * BR), BF),
            vmem((BC + 8, 3 * C, BR), BF),
            vmem((BC + 8, C, 2 * BR), F32),
            vmem((BC + 32, 3 * C, 2 * BR), BF),
            vmem((BC + 32, 3 * C, 2 * BR), BF),
            vmem((wide, 2 * C, 2 * BR), F32),
            vmem((wide, 3 * C, BR), BF),
            vmem((wide, 3 * C, BR), BF),
            vmem((wide, 3 * C, BR), BF),
            vmem((wide, 3 * C, BR), BF),
            vmem((BC + 16, 3 * C, 2 * BR), BF),
            vmem((BC + 8, 3 * C, BR), BF),
            vmem((BC, C, BR), BF),
            vmem((BC, C, BR), BF),
            vmem((BC, C, BR), BF),
            vmem((BC + 16, C, BR), BF),
            vmem((BC + 32, C, BR), BF),
            vmem((C, BC, BR), BF),
            vmem((C, BC, BR), BF),
        ]
    )
    whole = pl.BlockSpec(memory_space=pltpu.VMEM)
    anywhere = pl.BlockSpec(memory_space=pl.ANY)
    field = jax.ShapeDtypeStruct((C, BC, BR), BF)
    results = pl.pallas_call(
        functools.partial(main_kernel, nrow, ncol),
        out_shape=[field, field] + [jax.ShapeDtypeStruct(shape, F32) for shape in grad_shapes],
        in_specs=[anywhere] * 6,
        out_specs=[anywhere] * 4,
        scratch_shapes=scratch,
        compiler_params=pltpu.CompilerParams(
            collective_id=0, has_side_effects=True, vmem_limit_bytes=56 << 20
        ),
        name="blocks",
    )(*arrays)
    small = jax.ShapeDtypeStruct((3, 3, C, C), F32)
    return pl.pallas_call(
        finish_kernel,
        out_shape=[field, field, small, small, small, small],
        in_specs=[anywhere] * 4,
        out_specs=[whole] * 6,
        scratch_shapes=[vmem(shape, F32) for shape in grad_shapes]
        + [pltpu.SemaphoreType.DMA((4,))],
        compiler_params=pltpu.CompilerParams(vmem_limit_bytes=56 << 20),
        name="finish",
    )(*results)


def solution(mesh):
    return jax.shard_map(
        functools.partial(per_device, mesh.shape["row"], mesh.shape["col"]),
        mesh=mesh,
        in_specs=(P(None, "col", "row"), P(None, "col", "row"), P(), P(), P(), P()),
        out_specs=(P(None, "col", "row"), P(None, "col", "row"), P(), P(), P(), P()),
        check_vma=False,
    )
```

```python
import functools

import jax
import jax.numpy as jnp
from jax import lax
from jax.experimental import pallas as pl
from jax.experimental.pallas import tpu as pltpu
from jax.sharding import PartitionSpec as P

C = 32
BC = 32
BR = 128
DILATE_ONE = 4
DILATE_TWO = 8
MESH = pl.DeviceIdType.MESH
BF = jnp.bfloat16
F32 = jnp.float32


def dot(a, b):
    return jnp.dot(a, b, preferred_element_type=F32)


def permutation(inverse):
    row = lax.broadcasted_iota(jnp.int32, (256, 256), 0)
    col = lax.broadcasted_iota(jnp.int32, (256, 256), 1)
    if inverse:
        row, col = col, row
    same = (row // 8 == col % 32) & (row % 8 == col // 32)
    return jnp.where(same, 1.0, 0.0).astype(BF)


def fill_matrix(ref, row, kernel, flip, swap):
    for p in range(3):
        for q in range(3):
            a, b = (q, p) if swap else (p, q)
            if flip:
                piece = kernel[2 - a, 2 - b].astype(F32).T.astype(BF)
            else:
                piece = kernel[a, b]
            tap = 3 * p + q
            ref[row : row + C, tap * C : tap * C + C] = piece


def put_stack(ref, row, main, side, d, wide=False):
    lane = lax.broadcasted_iota(jnp.int32, (C, BR), 1)
    last = lane >= BR - d
    first = lane < d
    ref[row, 0:C, 0:BR] = pltpu.roll(jnp.where(last, side, main), d, 1)
    ref[row, C : 2 * C, 0:BR] = main
    ref[row, 2 * C : 3 * C, 0:BR] = pltpu.roll(jnp.where(first, side, main), BR - d, 1)
    if wide:
        ref[row, 0:C, BR : 2 * BR] = pltpu.roll(jnp.where(last, main, side), d, 1)
        ref[row, C : 2 * C, BR : 2 * BR] = side
        ref[row, 2 * C : 3 * C, BR : 2 * BR] = pltpu.roll(jnp.where(first, main, side), BR - d, 1)


def taps(ref, row, d):
    return jnp.concatenate([ref[row], ref[row + d], ref[row + 2 * d]], axis=0)


def rows(count, body, unroll=8, first=0):
    def step(t, carry):
        for u in range(unroll):
            body(first + t * unroll + u)
        return carry

    lax.fori_loop(0, count // unroll, step, 0)


def outer_rows(body, unroll):
    per = 16 // unroll

    def step(t, carry):
        for u in range(unroll):
            body(t * unroll + (t // per) * 16 + u)
        return carry

    lax.fori_loop(0, 2 * per, step, 0)


class Halo:
    names = ("own", "top", "bottom", "pack", "land", "send", "recv")

    def __init__(self, width, place, refs, by_way=False):
        self.h = width
        self.by_way = by_way
        self.per = BR // width
        self.edge = 16 // self.per
        self.count = BC // self.per
        self.place = place
        self.own, self.top, self.bottom, self.pack, self.land, self.send, self.recv = refs

    @staticmethod
    def scratch(width):
        per = BR // width
        return [
            pltpu.VMEM((BC, C, BR), BF),
            pltpu.VMEM((width, C, BR), BF),
            pltpu.VMEM((width, C, BR), BF),
            pltpu.VMEM((2, BC // per, C, BR), BF),
            pltpu.VMEM((2, 64 // per, C, BR), BF),
            pltpu.SemaphoreType.DMA((8,)),
            pltpu.SemaphoreType.DMA((8,)),
        ]

    def pieces(self):
        e, n, h = self.edge, self.count, self.h
        out = []
        for dr, dc, src, dst in (
            (0, -1, self.own.at[0:h], self.bottom),
            (0, 1, self.own.at[BC - h : BC], self.top),
            (-1, 0, self.pack.at[0], self.land.at[0, e : e + n]),
            (1, 0, self.pack.at[1], self.land.at[1, e : e + n]),
            (-1, -1, self.pack.at[0, 0:e], self.land.at[0, e + n :]),
            (-1, 1, self.pack.at[0, n - e : n], self.land.at[0, 0:e]),
            (1, -1, self.pack.at[1, 0:e], self.land.at[1, e + n :]),
            (1, 1, self.pack.at[1, n - e : n], self.land.at[1, 0:e]),
        ):
            target = (self.place.ri + dr, self.place.ci + dc)
            sends = self.place.inside(dr, dc)
            if self.by_way and dr and dc:
                side = 0 if dr < 0 else 1
                src = self.land.at[side, e : 2 * e] if dc < 0 else self.land.at[side, n : e + n]
                target = (self.place.ri, self.place.ci + dc)
                sends = self.place.inside(-dr, dc)
            out.append((dr, dc, src, dst, target, sends))
        return out

    def copy(self, k, piece):
        return pltpu.make_async_remote_copy(
            src_ref=piece[2],
            dst_ref=piece[3],
            send_sem=self.send.at[k],
            recv_sem=self.recv.at[k],
            device_id=piece[4],
            device_id_type=MESH,
        )

    def launch(self, which):
        for k, piece in enumerate(self.pieces()):
            if k in which:

                @pl.when(piece[5])
                def _():
                    self.copy(k, piece).start()

    def accept(self, which):
        for k, piece in enumerate(self.pieces()):
            if k in which:

                @pl.when(self.place.inside(-piece[0], -piece[1]))
                def _():
                    self.copy(k, piece).wait_recv()

    def start(self):
        self.launch((2, 3, 0, 1) if self.by_way else range(8))

    def forward(self):
        self.accept((2, 3))
        self.launch((4, 5, 6, 7))

    def wait(self):
        self.accept((0, 1, 4, 5, 6, 7) if self.by_way else range(8))

    def drain(self):
        for k, piece in enumerate(self.pieces()):

            @pl.when(piece[5])
            def _():
                self.copy(k, piece).wait_send()

    def fill_edges(self):
        for dr, dc, _, dst, _, _ in self.pieces():

            @pl.when(jnp.logical_not(self.place.inside(-dr, -dc)))
            def _():
                dst[...] = jnp.zeros(dst.shape, BF)

    def pack_sides(self):
        h, per = self.h, self.per
        group = lax.broadcasted_iota(jnp.int32, (C, BR), 1) // h

        def pack(t, carry):
            low = jnp.zeros((C, BR), BF)
            high = jnp.zeros((C, BR), BF)
            for j in range(per):
                v = self.own[t * per + j]
                turned = pltpu.roll(v, j * h, 1) if j else v
                low = jnp.where(group == j, turned, low)
                high = jnp.where(group == (j - 1) % per, turned, high)
            self.pack[0, t] = low
            self.pack[1, t] = high
            return carry

        lax.fori_loop(0, self.count, pack, 0)

    def prepare(self, ref, d):
        def own(k):
            main = self.own[k]
            ref[self.h + k, 0:C, 0:BR] = pltpu.roll(main, d, 1)
            ref[self.h + k, C : 2 * C, 0:BR] = main
            ref[self.h + k, 2 * C : 3 * C, 0:BR] = pltpu.roll(main, BR - d, 1)

        rows(BC, own, 16)

    def build(self, ref, d, inner=True, outer=True):
        h, per, e = self.h, self.per, self.edge
        lane = lax.broadcasted_iota(jnp.int32, (C, BR), 1)
        group = lane // h

        def complete(row, side):
            ref[row, C : 2 * C, BR : 2 * BR] = side
            for q, shift, edge in ((0, d, lane < d), (2, BR - d, lane >= BR - d)):
                there = ref[row, q * C : q * C + C, 0:BR]
                turned = pltpu.roll(side, shift, 1)
                ref[row, q * C : q * C + C, 0:BR] = jnp.where(edge, turned, there)
                ref[row, q * C : q * C + C, BR : 2 * BR] = jnp.where(edge, there, turned)

        def segment(main, first, pack, j0, nj, packs):
            def step(t, carry):
                low = self.land[0, pack + t]
                high = self.land[1, pack + t]
                for u in range(nj):
                    j = j0 + u
                    row = t * nj + u
                    side = jnp.where(
                        group == j,
                        low,
                        jnp.where(group == (j - 1) % per, high, jnp.zeros((C, BR), BF)),
                    )
                    if j:
                        side = pltpu.roll(side, BR - j * h, 1)
                    if main is self.own:
                        complete(first + row, side)
                    else:
                        put_stack(ref, first + row, main[row], side, d, True)
                return carry

            lax.fori_loop(0, packs, step, 0)

        nj = min(per, h)
        if inner:
            segment(self.own, h, e, 0, per, BC // per)
        if outer:
            segment(self.top, 0, 0, per - nj, nj, h // nj)
            segment(self.bottom, h + BC, e + BC // per, 0, nj, h // nj)


class Mirror:
    def __init__(self, place, refs):
        self.place = place
        self.n = place.nrow
        self.per = 8 // place.nrow
        self.ri = place.ri
        self.cq = place.ci // 4
        self.s = lax.rem(place.ci, 4)
        self.out, self.relay, self.land, self.send1, self.recv1, self.send2, self.recv2 = refs

    @staticmethod
    def scratch(nrow):
        return [
            pltpu.VMEM((8, BR, BR), BF),
            pltpu.VMEM((nrow, 8 // nrow, BR, BR), BF),
            pltpu.VMEM((4, 8, BC, BR), BF),
            pltpu.SemaphoreType.DMA((nrow,)),
            pltpu.SemaphoreType.DMA((nrow,)),
            pltpu.SemaphoreType.DMA((nrow, 4)),
            pltpu.SemaphoreType.DMA((4, nrow)),
        ]

    def relay_of(self, ri, cq, s, q):
        other = lax.rem(s + 2 * lax.rem(q + cq, 2), 4)
        return 2 * (q // 2) + lax.rem(ri, 2), 4 * (2 * (cq // 2) + lax.rem(q, 2)) + other

    def source(self, w):
        return (
            2 * (w // 2) + lax.rem(self.ri, 2),
            2 * (self.cq // 2) + lax.rem(w, 2),
            lax.rem(self.s + 2 * lax.rem(w + self.cq, 2), 4),
        )

    def my_w(self):
        return 2 * (self.ri // 2) + lax.rem(self.cq, 2)

    def my_q(self):
        return 2 * (self.ri // 2) + lax.rem(self.cq, 2)

    def first(self, q, w):
        return self.out.at[pl.ds(q * self.per, self.per)], self.relay.at[w], self.recv1.at[w]

    def second(self, w, k, slot, q):
        r0 = pl.multiple_of(k * BC, BC)
        return (
            self.relay.at[w, :, pl.ds(r0, BC)],
            self.land.at[slot, pl.ds(q * self.per, self.per)],
            self.recv2.at[slot, q],
        )

    def target1(self, q):
        return self.relay_of(self.ri, self.cq, self.s, q)

    def target2(self, w, k):
        ri, cq, _ = self.source(w)
        return cq, 4 * ri + k

    def is_self(self, device):
        return (device[0] == self.ri) & (device[1] == self.place.ci)

    def copy(self, parts, send, device):
        src, dst, recv = parts
        return pltpu.make_async_remote_copy(
            src_ref=src, dst_ref=dst, send_sem=send, recv_sem=recv, device_id=device, device_id_type=MESH
        )

    def go(self, parts, send, device):
        here = self.is_self(device)

        @pl.when(here)
        def _():
            pltpu.make_async_copy(*parts).start()

        @pl.when(jnp.logical_not(here))
        def _():
            self.copy(parts, send, device).start()

    def arrived(self, parts, send):
        self.copy(parts, send, (self.ri, self.place.ci)).wait_recv()

    def start(self):
        w = self.my_w()

        def step(q, carry):
            self.go(self.first(q, w), self.send1.at[q], self.target1(q))
            return carry

        lax.fori_loop(0, self.n, step, 0)

    def forward(self):
        mine = self.my_q()

        def step(w, carry):
            self.arrived(self.first(0, w), self.send1.at[0])
            slot = self.source(w)[2]
            for k in range(4):
                self.go(self.second(w, k, slot, mine), self.send2.at[w, k], self.target2(w, k))
            return carry

        lax.fori_loop(0, self.n, step, 0)

    def wait(self):
        def step(q, carry):
            for k in range(4):
                self.arrived(self.second(0, 0, k, q), self.send2.at[0, 0])
            return carry

        lax.fori_loop(0, self.n, step, 0)

    def drain(self):
        def step(q, carry):
            @pl.when(jnp.logical_not(self.is_self(self.target1(q))))
            def _():
                self.copy(self.first(q, 0), self.send1.at[q], self.target1(q)).wait_send()

            for k in range(4):

                @pl.when(jnp.logical_not(self.is_self(self.target2(q, k))))
                def _():
                    self.copy(self.second(q, k, 0, 0), self.send2.at[q, k], self.target2(q, k)).wait_send()

            return carry

        lax.fori_loop(0, self.n, step, 0)

    def greet(self, greet):
        def step(q, count):
            ri, cq, s = self.source(q)
            source = ri, 4 * cq + s

            @pl.when(jnp.logical_not(self.is_self(source)))
            def _():
                greet(*source)

            count = count + jnp.logical_not(self.is_self(self.target1(q))).astype(jnp.int32)
            for k in range(4):
                relay = self.relay_of(self.cq, self.ri, k, q)

                @pl.when(jnp.logical_not(self.is_self(relay)))
                def _():
                    greet(*relay)

                away = jnp.logical_not(self.is_self(self.target2(q, k)))
                count = count + away.astype(jnp.int32)
            return count

        return lax.fori_loop(0, self.n, step, jnp.int32(0))

    def fetch(self):
        lane = lax.broadcasted_iota(jnp.int32, (8, BC, BR), 2)
        half = lane < 64
        even = (lane // 32) % 2 == 0
        l0, l1, l2, l3 = (self.land[k] for k in range(4))
        a0 = jnp.where(half, l0, pltpu.roll(l2, 64, 2))
        a2 = jnp.where(half, pltpu.roll(l0, 64, 2), l2)
        a1 = jnp.where(half, l1, pltpu.roll(l3, 64, 2))
        a3 = jnp.where(half, pltpu.roll(l1, 64, 2), l3)
        return (
            jnp.where(even, a0, pltpu.roll(a1, 32, 2)),
            jnp.where(even, pltpu.roll(a0, 96, 2), a1),
            jnp.where(even, a2, pltpu.roll(a3, 32, 2)),
            jnp.where(even, pltpu.roll(a2, 96, 2), a3),
        )


class Place:
    def __init__(self, nrow, ncol):
        self.nrow = nrow
        self.ncol = ncol
        self.ri = lax.axis_index("row")
        self.ci = lax.axis_index("col")

    def inside(self, dr, dc):
        ok = None
        for index, step, size in ((self.ri, dr, self.nrow), (self.ci, dc, self.ncol)):
            if step:
                here = index < size - 1 if step > 0 else index > 0
                ok = here if ok is None else ok & here
        return ok


def interleave(groups):
    return jnp.concatenate(groups, axis=1)


class Total:
    def __init__(self, place, refs):
        self.place = place
        self.acc, self.r1, self.mine, self.r2, self.fin = refs[:5]
        self.send1, self.recv1, self.send2, self.recv2, self.send3, self.recv3 = refs[5:]
        self.owners = self.acc.shape[0]
        self.n1 = place.ncol // 2
        self.n2 = 2 * place.nrow
        self.a = lax.rem(place.ci, self.n1)
        self.half = place.ci // self.n1
        self.m = place.ri * 2 + self.half
        self.owner = self.a < self.owners

    @staticmethod
    def scratch(n1, n2, owners, count):
        block = (count, 3 * C // owners, BR)
        vmem = pltpu.VMEM
        return [
            vmem((owners,) + block, F32),
            vmem((n1,) + block, F32),
            vmem(block, F32),
            vmem((n2,) + block, F32),
            vmem((owners,) + block, F32),
        ] + [pltpu.SemaphoreType.DMA((n,)) for n in (owners, n1, n2, n2, n1, owners)]

    def group1(self, b):
        return self.place.ri, self.half * self.n1 + b

    def group2(self, m):
        return m // 2, lax.rem(m, 2) * self.n1 + self.a

    def others(self, count, me, body):
        def step(b, carry):
            @pl.when(b != me)
            def _():
                body(b)

            return carry

        lax.fori_loop(0, count, step, 0)

    def share(self, src, dst, send, recv, device):
        return pltpu.make_async_remote_copy(
            src_ref=src, dst_ref=dst, send_sem=send, recv_sem=recv, device_id=device, device_id_type=MESH
        )

    def scatter(self, b, slot):
        return self.share(
            self.acc.at[b], self.r1.at[slot], self.send1.at[b], self.recv1.at[slot], self.group1(b)
        )

    def spread(self, m, slot):
        return self.share(
            self.mine, self.r2.at[slot], self.send2.at[m], self.recv2.at[slot], self.group2(m)
        )

    def gather(self, b, src, slot):
        return self.share(
            self.fin.at[src], self.fin.at[slot], self.send3.at[b], self.recv3.at[slot], self.group1(b)
        )

    def start1(self):
        self.others(self.owners, self.a, lambda b: self.scatter(b, self.a).start())

    def start2(self):
        @pl.when(self.owner)
        def _():
            self.r1[self.a] = self.acc[self.a]
            self.others(self.n1, self.a, lambda b: self.scatter(0, b).wait_recv())
            self.mine[...] = sum(self.r1[b] for b in range(self.n1))
            self.others(self.n2, self.m, lambda m: self.spread(m, self.m).start())
            self.r2[self.m] = self.mine[...]

    def start3(self):
        @pl.when(self.owner)
        def _():
            self.others(self.n2, self.m, lambda m: self.spread(m, m).wait_recv())
            self.fin[self.a] = sum(self.r2[m] for m in range(self.n2))
            self.others(self.n1, self.a, lambda b: self.gather(b, self.a, self.a).start())

    def finish(self):
        self.others(self.owners, self.a, lambda b: self.gather(0, 0, b).wait_recv())

    def drain(self):
        self.others(self.owners, self.a, lambda b: self.scatter(b, 0).wait_send())

        @pl.when(self.owner)
        def _():
            self.others(self.n2, self.m, lambda m: self.spread(m, 0).wait_send())
            self.others(self.n1, self.a, lambda b: self.gather(b, self.a, 0).wait_send())


def kernel_grad(padding, own, stacked, d, out, which):
    def fill(k):
        padding[k + 2 * d] = own(k)

    rows(BC, fill, 16)
    total = jnp.zeros((3 * C, 3 * C), F32)
    for t in range((BC + 2 * d) // 8):
        left = []
        right = []
        for k in range(t * 8, t * 8 + 8):
            left.append(
                jnp.concatenate([padding[k + 2 * d], padding[k + d], padding[k]], axis=0)
            )
            right.append(stacked[k, :, 0:BR])
        total = total + lax.dot_general(
            jnp.concatenate(left, axis=1),
            jnp.concatenate(right, axis=1),
            (((1,), (1,)), ((), ())),
            preferred_element_type=F32,
        )
    per = out.shape[2]
    for t in range(3 * C // per):
        out[t, which, :, 0 : 3 * C] = total[t * per : t * per + per]


def main_kernel(nrow, ncol, *refs):
    inputs, (dec_out, g0_out, early_out, late_out) = refs[:6], refs[6:10]
    rest = list(refs[10:])

    def take(n):
        out = rest[:n]
        del rest[:n]
        return out

    place = Place(nrow, ncol)
    ri, ci = place.ri, place.ci
    halo_x = Halo(8, place, take(7), True)
    halo_s2 = Halo(16, place, take(7), True)
    halo_z = Halo(16, place, take(7), True)
    halo_s1 = Halo(8, place, take(7))
    halos = (halo_x, halo_s2, halo_z, halo_s1)
    mir_g = Mirror(place, take(7))
    mir_y = Mirror(place, take(7))
    early = Total(place, take(11))
    late = Total(place, take(11))
    held = take(6)
    x_ref, g_ref, fa, fb, sa, sb = held
    in_sem, out_sem = take(2)
    (wa1, wb1, wa2, wb2, wb2t, tb2, ta2, ta2t, tb1, ta1) = take(10)
    (xc1, hc1, slope1, xc2, sc2, hg2, hc2, hc2t, ec2, ec2t, sc1, ec1, y1, dec, g0) = take(15)
    pad1, pad2, dec_nat, g0_nat = take(4)

    loads = [
        pltpu.make_async_copy(src, dst, in_sem.at[k]) for k, (src, dst) in enumerate(zip(inputs, held))
    ]
    for load in loads:
        load.start()

    barrier = pltpu.get_barrier_semaphore()
    expected = jnp.int32(early.n1 + early.n2 - 2)

    def greet(row, col):
        pl.semaphore_signal(barrier, inc=1, device_id=(row, col), device_id_type=MESH)

    for dr in (-1, 0, 1):
        for dc in (-1, 0, 1):
            if dr or dc:
                ok = place.inside(dr, dc)
                expected = expected + ok.astype(jnp.int32)

                @pl.when(ok)
                def _():
                    greet(ri + dr, ci + dc)

    expected = expected + mir_g.greet(greet)
    early.others(early.n1, early.a, lambda b: greet(*early.group1(b)))
    early.others(early.n2, early.m, lambda m: greet(*early.group2(m)))

    order = permutation(False)
    loads[0].wait()
    flat = x_ref[...].reshape(C * BC, BR)
    halo_x.own[...] = interleave(
        [dot(order, flat[256 * t : 256 * t + 256]).reshape(BC, 8, BR) for t in range(4)]
    ).astype(BF)
    halo_x.pack_sides()
    for load in loads[1:]:
        load.wait()
    gflat = g_ref[...].reshape(C * BC, BR)
    for j in range(8):
        mir_g.out[j] = gflat[j * BR : j * BR + BR].T
    fill_matrix(wa1, 0, fa, False, False)
    fill_matrix(wb1, 0, fb, False, False)
    pl.semaphore_wait(barrier, expected)
    halo_x.start()
    mir_g.start()

    fill_matrix(wa2, 0, sa, False, False)
    fill_matrix(wa2, C, sa, False, True)
    fill_matrix(wb2, 0, sb, False, False)
    fill_matrix(wb2t, 0, sb, False, True)
    fill_matrix(tb2, 0, sb, True, False)
    fill_matrix(tb2, C, sb, True, True)
    fill_matrix(ta2, 0, sa, True, False)
    fill_matrix(ta2t, 0, sa, True, True)
    fill_matrix(tb1, 0, fb, True, False)
    fill_matrix(ta1, 0, fa, True, False)
    for halo in halos:
        halo.fill_edges()
    for ref in (pad1, pad2, early.acc, late.acc):
        ref[...] = jnp.zeros(ref.shape, ref.dtype)

    lane = lax.broadcasted_iota(jnp.int32, (C, BR), 1)
    first_lane = jnp.where(ri < nrow - 1, 0, 64)
    last_lane = jnp.where(ri > 0, BR, 64)
    side_ok = (lane >= first_lane) & (lane < last_lane)

    def put_field(ref, k, d, v):
        bin_index = ci * BC + k - d
        ok = (bin_index >= 0) & (bin_index < ncol * BC)
        main = jnp.where(ok, v[:, :BR], 0.0).astype(BF)
        side = jnp.where(side_ok & ok, v[:, BR:], 0.0).astype(BF)
        put_stack(ref, k, main, side, d)

    d = DILATE_ONE
    halo_x.prepare(xc1, d)
    halo_x.forward()
    mir_g.forward()
    halo_x.build(xc1, d, outer=False)

    def hidden1(k):
        pre = dot(wa1[...], taps(xc1, k, d))
        sig = jax.nn.sigmoid(pre)
        slope1[k] = sig * (1.0 + pre * (1.0 - sig))
        put_field(hc1, k, d, pre * sig)

    rows(24, hidden1, 12, 8)
    halo_x.wait()
    halo_x.build(xc1, d, inner=False)

    def edge1(t, carry):
        for u in range(8):
            hidden1(t * 32 + u)
        return carry

    lax.fori_loop(0, 2, edge1, 0)

    def outer1(k):
        y1[k] = (halo_x.own[k].astype(F32) + dot(wb1[...], taps(hc1, k, d))).astype(BF)

    rows(BC, outer1, 16)

    back = permutation(True)
    for t in range(4):
        part = y1[:, 8 * t : 8 * t + 8, :].reshape(256, BR)
        natural = dot(back, part)
        for j in range(2):
            mir_y.out[2 * t + j] = natural[j * BR : j * BR + BR].T.astype(BF)
    mir_y.start()
    mir_y.forward()

    mir_g.wait()
    turned = mir_g.fetch()
    parts = []
    for t in range(4):
        mirrored = jnp.concatenate(
            [turned[n][2 * t + j] for j in range(2) for n in range(4)], axis=0
        )
        here = gflat[256 * t : 256 * t + 256]
        mean = ((here.astype(F32) + mirrored.astype(F32)) * 0.5).astype(BF)
        parts.append(dot(order, mean).reshape(BC, 8, BR))
    halo_s2.own[...] = interleave(parts).astype(BF)
    halo_s2.pack_sides()
    halo_s2.start()
    halo_s2.prepare(sc2, DILATE_TWO)

    mir_y.wait()
    turned = mir_y.fetch()
    parts = []
    for t in range(4):
        mirrored = jnp.concatenate(
            [turned[n][2 * t + j] for j in range(2) for n in range(4)], axis=0
        )
        parts.append(dot(order, mirrored).reshape(BC, 8, BR))
    halo_z.own[...] = ((y1[...].astype(F32) + interleave(parts)) * 0.5).astype(BF)
    halo_z.pack_sides()
    halo_z.start()
    halo_s2.forward()
    halo_s2.build(sc2, DILATE_TWO, outer=False)
    halo_z.prepare(xc2, DILATE_TWO)

    d = DILATE_TWO

    def cotangent2(k):
        hg2[k] = dot(tb2[...], taps(sc2, k, d))

    halo_s2.wait()
    halo_s2.build(sc2, d, inner=False)
    rows(BC + 2 * d, cotangent2, 16)
    halo_z.forward()
    halo_z.build(xc2, d, outer=False)

    def hidden2(k):
        pre = dot(wa2[...], taps(xc2, k, d))
        sig = jax.nn.sigmoid(pre)
        hid = pre * sig
        grad = hg2[k] * (sig * (1.0 + pre * (1.0 - sig)))
        hg2[k] = hid
        put_field(ec2, k, d, grad[:C])
        put_field(ec2t, k, d, grad[C:])

    rows(16, hidden2, 8, 16)
    halo_z.wait()
    halo_z.build(xc2, d, inner=False)
    outer_rows(hidden2, 8)

    def upstream1(k):
        base = halo_s2.own[k].astype(F32)
        one = (base + dot(ta2[...], taps(ec2, k, d))).astype(BF)
        two = (base + dot(ta2t[...], taps(ec2t, k, d))).astype(BF)
        halo_s1.own[k] = ((one.astype(F32) + two.astype(F32)) * 0.5).astype(BF)

    rows(BC, upstream1, 16)
    halo_s1.pack_sides()
    halo_s1.start()
    halo_s1.prepare(sc1, DILATE_ONE)

    def place2(k):
        put_field(hc2, k, DILATE_TWO, hg2[k, :C, :])

    rows(BC + 2 * d, place2)
    kernel_grad(pad2, lambda k: halo_s2.own[k], hc2, d, early.acc, 2)
    kernel_grad(
        pad2, lambda k: ec2[k + DILATE_TWO, C : 2 * C, :], xc2.at[d : d + BC + 2 * d], d, early.acc, 1
    )

    d = DILATE_ONE
    kernel_grad(pad1, lambda k: halo_s1.own[k], hc1, d, early.acc, 0)
    early.start1()
    halo_s1.wait()
    halo_s1.build(sc1, d)

    def cotangent1(k):
        put_field(ec1, k, d, dot(tb1[...], taps(sc1, k, d)) * slope1[k])

    rows(BC + 2 * d, cotangent1, 10)
    kernel_grad(
        pad1, lambda k: ec1[k + DILATE_ONE, C : 2 * C, :], xc1.at[d : d + BC + 2 * d], d, late.acc, 0
    )
    late.start1()
    early.start2()

    def by_channel(src, dst):
        for t in range(4):
            part = src[:, 8 * t : 8 * t + 8, :].reshape(256, BR)
            dst[8 * t : 8 * t + 8] = dot(back, part).astype(BF).reshape(8, BC, BR)

    def upstream0(k):
        g0[k] = (halo_s1.own[k].astype(F32) + dot(ta1[...], taps(ec1, k, d))).astype(BF)

    rows(BC, upstream0, 16)
    by_channel(g0, g0_nat)
    g0_copy = pltpu.make_async_copy(g0_nat, g0_out, out_sem.at[0])
    g0_copy.start()
    late.start2()

    def place2t(k):
        put_field(hc2t, k, DILATE_TWO, hg2[k, C:, :])

    rows(BC + 16, place2t)

    def outer2(k):
        base = halo_z.own[k].astype(F32)
        one = (base + dot(wb2[...], taps(hc2, k, DILATE_TWO))).astype(BF)
        two = (base + dot(wb2t[...], taps(hc2t, k, DILATE_TWO))).astype(BF)
        dec[k] = ((one.astype(F32) + two.astype(F32)) * 0.5).astype(BF)

    rows(BC, outer2, 16)
    by_channel(dec, dec_nat)
    dec_copy = pltpu.make_async_copy(dec_nat, dec_out, out_sem.at[1])
    dec_copy.start()
    early.start3()
    late.start3()
    for halo in halos:
        halo.drain()
    mir_g.drain()
    mir_y.drain()
    early.finish()
    early_copy = pltpu.make_async_copy(early.fin, early_out, out_sem.at[2])
    early_copy.start()
    late.finish()
    late_copy = pltpu.make_async_copy(late.fin, late_out, out_sem.at[3])
    late_copy.start()
    early.drain()
    late.drain()
    for copy in (g0_copy, dec_copy, early_copy, late_copy):
        copy.wait()


def finish_kernel(dec_in, g0_in, early_in, late_in, out_dec, out_g0, out_a1, out_b1, out_a2, out_b2, early, late, sems):
    copies = [
        pltpu.make_async_copy(src, dst, sems.at[k])
        for k, (src, dst) in enumerate(
            ((late_in, late), (early_in, early), (dec_in, out_dec), (g0_in, out_g0))
        )
    ]
    for copy in copies:
        copy.start()
    copies[0].wait()
    copies[1].wait()
    owners = early.shape[0]
    for src, which, dst in ((late, 0, out_a1), (early, 0, out_b1), (early, 1, out_a2), (early, 2, out_b2)):
        band = src[:, which].reshape(3 * C, BR)
        for p in range(3):
            for q in range(3):
                dst[p, q] = band[p * C : p * C + C, q * C : q * C + C]
    copies[2].wait()
    copies[3].wait()


def per_device(nrow, ncol, *arrays):
    n1 = ncol // 2
    n2 = 2 * nrow
    owners = 12 if n1 >= 12 else 4
    wide = BC + 16
    vmem = pltpu.VMEM
    grad_shapes = [(owners, count, 3 * C // owners, BR) for count in (3, 1)]
    scratch = (
        Halo.scratch(8)
        + Halo.scratch(16)
        + Halo.scratch(16)
        + Halo.scratch(8)
        + Mirror.scratch(nrow)
        + Mirror.scratch(nrow)
        + Total.scratch(n1, n2, owners, 3)
        + Total.scratch(n1, n2, owners, 1)
        + [vmem((C, BC, BR), BF)] * 2
        + [vmem((3, 3, C, C), BF)] * 4
        + [pltpu.SemaphoreType.DMA((6,)), pltpu.SemaphoreType.DMA((4,))]
        + [vmem((m, 9 * C), BF) for m in (C, C, 2 * C, C, C, 2 * C, C, C, C, C)]
        + [
            vmem((BC + 16, 3 * C, 2 * BR), BF),
            vmem((BC + 8, 3 * C, BR), BF),
            vmem((BC + 8, C, 2 * BR), F32),
            vmem((BC + 32, 3 * C, 2 * BR), BF),
            vmem((BC + 32, 3 * C, 2 * BR), BF),
            vmem((wide, 2 * C, 2 * BR), F32),
            vmem((wide, 3 * C, BR), BF),
            vmem((wide, 3 * C, BR), BF),
            vmem((wide, 3 * C, BR), BF),
            vmem((wide, 3 * C, BR), BF),
            vmem((BC + 16, 3 * C, 2 * BR), BF),
            vmem((BC + 8, 3 * C, BR), BF),
            vmem((BC, C, BR), BF),
            vmem((BC, C, BR), BF),
            vmem((BC, C, BR), BF),
            vmem((BC + 16, C, BR), BF),
            vmem((BC + 32, C, BR), BF),
            vmem((C, BC, BR), BF),
            vmem((C, BC, BR), BF),
        ]
    )
    whole = pl.BlockSpec(memory_space=pltpu.VMEM)
    anywhere = pl.BlockSpec(memory_space=pl.ANY)
    field = jax.ShapeDtypeStruct((C, BC, BR), BF)
    results = pl.pallas_call(
        functools.partial(main_kernel, nrow, ncol),
        out_shape=[field, field] + [jax.ShapeDtypeStruct(shape, F32) for shape in grad_shapes],
        in_specs=[anywhere] * 6,
        out_specs=[anywhere] * 4,
        scratch_shapes=scratch,
        compiler_params=pltpu.CompilerParams(
            collective_id=0, has_side_effects=True, vmem_limit_bytes=56 << 20
        ),
        name="blocks",
    )(*arrays)
    small = jax.ShapeDtypeStruct((3, 3, C, C), F32)
    return pl.pallas_call(
        finish_kernel,
        out_shape=[field, field, small, small, small, small],
        in_specs=[anywhere] * 4,
        out_specs=[whole] * 6,
        scratch_shapes=[vmem(shape, F32) for shape in grad_shapes]
        + [pltpu.SemaphoreType.DMA((4,))],
        compiler_params=pltpu.CompilerParams(vmem_limit_bytes=56 << 20),
        name="finish",
    )(*results)


def solution(mesh):
    return jax.shard_map(
        functools.partial(per_device, mesh.shape["row"], mesh.shape["col"]),
        mesh=mesh,
        in_specs=(P(None, "col", "row"), P(None, "col", "row"), P(), P(), P(), P()),
        out_specs=(P(None, "col", "row"), P(None, "col", "row"), P(), P(), P(), P()),
        check_vma=False,
    )
```

```python
import functools

import jax
import jax.numpy as jnp
from jax import lax
from jax.experimental import pallas as pl
from jax.experimental.pallas import tpu as pltpu
from jax.sharding import PartitionSpec as P

C = 32
BC = 32
BR = 128
DILATE_ONE = 4
DILATE_TWO = 8
MESH = pl.DeviceIdType.MESH
BF = jnp.bfloat16
F32 = jnp.float32


def dot(a, b):
    return jnp.dot(a, b, preferred_element_type=F32)


def permutation(inverse):
    row = lax.broadcasted_iota(jnp.int32, (256, 256), 0)
    col = lax.broadcasted_iota(jnp.int32, (256, 256), 1)
    if inverse:
        row, col = col, row
    same = (row // 8 == col % 32) & (row % 8 == col // 32)
    return jnp.where(same, 1.0, 0.0).astype(BF)


def fill_matrix(ref, row, kernel, flip, swap):
    for p in range(3):
        for q in range(3):
            a, b = (q, p) if swap else (p, q)
            if flip:
                piece = kernel[2 - a, 2 - b].astype(F32).T.astype(BF)
            else:
                piece = kernel[a, b]
            tap = 3 * p + q
            ref[row : row + C, tap * C : tap * C + C] = piece


def put_stack(ref, row, main, side, d, wide=False):
    lane = lax.broadcasted_iota(jnp.int32, (C, BR), 1)
    last = lane >= BR - d
    first = lane < d
    ref[row, 0:C, 0:BR] = pltpu.roll(jnp.where(last, side, main), d, 1)
    ref[row, C : 2 * C, 0:BR] = main
    ref[row, 2 * C : 3 * C, 0:BR] = pltpu.roll(jnp.where(first, side, main), BR - d, 1)
    if wide:
        ref[row, 0:C, BR : 2 * BR] = pltpu.roll(jnp.where(last, main, side), d, 1)
        ref[row, C : 2 * C, BR : 2 * BR] = side
        ref[row, 2 * C : 3 * C, BR : 2 * BR] = pltpu.roll(jnp.where(first, main, side), BR - d, 1)


def taps(ref, row, d):
    return jnp.concatenate([ref[row], ref[row + d], ref[row + 2 * d]], axis=0)


def rows(count, body, unroll=8, first=0):
    def step(t, carry):
        for u in range(unroll):
            body(first + t * unroll + u)
        return carry

    lax.fori_loop(0, count // unroll, step, 0)


def outer_rows(body, unroll):
    per = 16 // unroll

    def step(t, carry):
        for u in range(unroll):
            body(t * unroll + (t // per) * 16 + u)
        return carry

    lax.fori_loop(0, 2 * per, step, 0)


class Halo:
    names = ("own", "top", "bottom", "pack", "land", "send", "recv")

    def __init__(self, width, place, refs, by_way=False):
        self.h = width
        self.by_way = by_way
        self.per = BR // width
        self.edge = 16 // self.per
        self.count = BC // self.per
        self.place = place
        self.own, self.top, self.bottom, self.pack, self.land, self.send, self.recv = refs

    @staticmethod
    def scratch(width):
        per = BR // width
        return [
            pltpu.VMEM((BC, C, BR), BF),
            pltpu.VMEM((width, C, BR), BF),
            pltpu.VMEM((width, C, BR), BF),
            pltpu.VMEM((2, BC // per, C, BR), BF),
            pltpu.VMEM((2, 64 // per, C, BR), BF),
            pltpu.SemaphoreType.DMA((8,)),
            pltpu.SemaphoreType.DMA((8,)),
        ]

    def pieces(self):
        e, n, h = self.edge, self.count, self.h
        out = []
        for dr, dc, src, dst in (
            (0, -1, self.own.at[0:h], self.bottom),
            (0, 1, self.own.at[BC - h : BC], self.top),
            (-1, 0, self.pack.at[0], self.land.at[0, e : e + n]),
            (1, 0, self.pack.at[1], self.land.at[1, e : e + n]),
            (-1, -1, self.pack.at[0, 0:e], self.land.at[0, e + n :]),
            (-1, 1, self.pack.at[0, n - e : n], self.land.at[0, 0:e]),
            (1, -1, self.pack.at[1, 0:e], self.land.at[1, e + n :]),
            (1, 1, self.pack.at[1, n - e : n], self.land.at[1, 0:e]),
        ):
            target = (self.place.ri + dr, self.place.ci + dc)
            sends = self.place.inside(dr, dc)
            if self.by_way and dr and dc:
                side = 0 if dr < 0 else 1
                src = self.land.at[side, e : 2 * e] if dc < 0 else self.land.at[side, n : e + n]
                target = (self.place.ri, self.place.ci + dc)
                sends = self.place.inside(-dr, dc)
            out.append((dr, dc, src, dst, target, sends))
        return out

    def copy(self, k, piece):
        return pltpu.make_async_remote_copy(
            src_ref=piece[2],
            dst_ref=piece[3],
            send_sem=self.send.at[k],
            recv_sem=self.recv.at[k],
            device_id=piece[4],
            device_id_type=MESH,
        )

    def launch(self, which):
        for k, piece in enumerate(self.pieces()):
            if k in which:

                @pl.when(piece[5])
                def _():
                    self.copy(k, piece).start()

    def accept(self, which):
        for k, piece in enumerate(self.pieces()):
            if k in which:

                @pl.when(self.place.inside(-piece[0], -piece[1]))
                def _():
                    self.copy(k, piece).wait_recv()

    def start(self):
        self.launch((2, 3, 0, 1) if self.by_way else range(8))

    def forward(self):
        self.accept((2, 3))
        self.launch((4, 5, 6, 7))

    def wait(self):
        self.accept((0, 1, 4, 5, 6, 7) if self.by_way else range(8))

    def drain(self):
        for k, piece in enumerate(self.pieces()):

            @pl.when(piece[5])
            def _():
                self.copy(k, piece).wait_send()

    def fill_edges(self):
        for dr, dc, _, dst, _, _ in self.pieces():

            @pl.when(jnp.logical_not(self.place.inside(-dr, -dc)))
            def _():
                dst[...] = jnp.zeros(dst.shape, BF)

    def pack_sides(self):
        h, per = self.h, self.per
        group = lax.broadcasted_iota(jnp.int32, (C, BR), 1) // h

        def pack(t, carry):
            low = jnp.zeros((C, BR), BF)
            high = jnp.zeros((C, BR), BF)
            for j in range(per):
                v = self.own[t * per + j]
                turned = pltpu.roll(v, j * h, 1) if j else v
                low = jnp.where(group == j, turned, low)
                high = jnp.where(group == (j - 1) % per, turned, high)
            self.pack[0, t] = low
            self.pack[1, t] = high
            return carry

        lax.fori_loop(0, self.count, pack, 0)

    def prepare(self, ref, d):
        def own(k):
            main = self.own[k]
            ref[self.h + k, 0:C, 0:BR] = pltpu.roll(main, d, 1)
            ref[self.h + k, C : 2 * C, 0:BR] = main
            ref[self.h + k, 2 * C : 3 * C, 0:BR] = pltpu.roll(main, BR - d, 1)

        rows(BC, own, 16)

    def build(self, ref, d, inner=True, outer=True):
        h, per, e = self.h, self.per, self.edge
        lane = lax.broadcasted_iota(jnp.int32, (C, BR), 1)
        group = lane // h

        def complete(row, side):
            ref[row, C : 2 * C, BR : 2 * BR] = side
            for q, shift, edge in ((0, d, lane < d), (2, BR - d, lane >= BR - d)):
                there = ref[row, q * C : q * C + C, 0:BR]
                turned = pltpu.roll(side, shift, 1)
                ref[row, q * C : q * C + C, 0:BR] = jnp.where(edge, turned, there)
                ref[row, q * C : q * C + C, BR : 2 * BR] = jnp.where(edge, there, turned)

        def segment(main, first, pack, j0, nj, packs):
            def step(t, carry):
                low = self.land[0, pack + t]
                high = self.land[1, pack + t]
                for u in range(nj):
                    j = j0 + u
                    row = t * nj + u
                    side = jnp.where(
                        group == j,
                        low,
                        jnp.where(group == (j - 1) % per, high, jnp.zeros((C, BR), BF)),
                    )
                    if j:
                        side = pltpu.roll(side, BR - j * h, 1)
                    if main is self.own:
                        complete(first + row, side)
                    else:
                        put_stack(ref, first + row, main[row], side, d, True)
                return carry

            lax.fori_loop(0, packs, step, 0)

        nj = min(per, h)
        if inner:
            segment(self.own, h, e, 0, per, BC // per)
        if outer:
            segment(self.top, 0, 0, per - nj, nj, h // nj)
            segment(self.bottom, h + BC, e + BC // per, 0, nj, h // nj)


class Mirror:
    def __init__(self, place, refs):
        self.place = place
        self.n = place.nrow
        self.per = 8 // place.nrow
        self.ri = place.ri
        self.cq = place.ci // 4
        self.s = lax.rem(place.ci, 4)
        self.out, self.relay, self.land, self.send1, self.recv1, self.send2, self.recv2 = refs

    @staticmethod
    def scratch(nrow):
        return [
            pltpu.VMEM((8, BR, BR), BF),
            pltpu.VMEM((nrow, 8 // nrow, BR, BR), BF),
            pltpu.VMEM((4, 8, BC, BR), BF),
            pltpu.SemaphoreType.DMA((nrow,)),
            pltpu.SemaphoreType.DMA((nrow,)),
            pltpu.SemaphoreType.DMA((nrow, 4)),
            pltpu.SemaphoreType.DMA((4, nrow)),
        ]

    def relay_of(self, ri, cq, s, q):
        other = lax.rem(s + 2 * lax.rem(q + cq, 2), 4)
        return 2 * (q // 2) + lax.rem(ri, 2), 4 * (2 * (cq // 2) + lax.rem(q, 2)) + other

    def source(self, w):
        return (
            2 * (w // 2) + lax.rem(self.ri, 2),
            2 * (self.cq // 2) + lax.rem(w, 2),
            lax.rem(self.s + 2 * lax.rem(w + self.cq, 2), 4),
        )

    def my_w(self):
        return 2 * (self.ri // 2) + lax.rem(self.cq, 2)

    def my_q(self):
        return 2 * (self.ri // 2) + lax.rem(self.cq, 2)

    def first(self, q, w):
        return self.out.at[pl.ds(q * self.per, self.per)], self.relay.at[w], self.recv1.at[w]

    def second(self, w, k, slot, q):
        r0 = pl.multiple_of(k * BC, BC)
        return (
            self.relay.at[w, :, pl.ds(r0, BC)],
            self.land.at[slot, pl.ds(q * self.per, self.per)],
            self.recv2.at[slot, q],
        )

    def target1(self, q):
        return self.relay_of(self.ri, self.cq, self.s, q)

    def target2(self, w, k):
        ri, cq, _ = self.source(w)
        return cq, 4 * ri + k

    def is_self(self, device):
        return (device[0] == self.ri) & (device[1] == self.place.ci)

    def copy(self, parts, send, device):
        src, dst, recv = parts
        return pltpu.make_async_remote_copy(
            src_ref=src, dst_ref=dst, send_sem=send, recv_sem=recv, device_id=device, device_id_type=MESH
        )

    def go(self, parts, send, device):
        here = self.is_self(device)

        @pl.when(here)
        def _():
            pltpu.make_async_copy(*parts).start()

        @pl.when(jnp.logical_not(here))
        def _():
            self.copy(parts, send, device).start()

    def arrived(self, parts, send):
        self.copy(parts, send, (self.ri, self.place.ci)).wait_recv()

    def start(self):
        w = self.my_w()

        def step(q, carry):
            self.go(self.first(q, w), self.send1.at[q], self.target1(q))
            return carry

        lax.fori_loop(0, self.n, step, 0)

    def forward(self):
        mine = self.my_q()

        def step(w, carry):
            self.arrived(self.first(0, w), self.send1.at[0])
            slot = self.source(w)[2]
            for k in range(4):
                self.go(self.second(w, k, slot, mine), self.send2.at[w, k], self.target2(w, k))
            return carry

        lax.fori_loop(0, self.n, step, 0)

    def wait(self):
        def step(q, carry):
            for k in range(4):
                self.arrived(self.second(0, 0, k, q), self.send2.at[0, 0])
            return carry

        lax.fori_loop(0, self.n, step, 0)

    def drain(self):
        def step(q, carry):
            @pl.when(jnp.logical_not(self.is_self(self.target1(q))))
            def _():
                self.copy(self.first(q, 0), self.send1.at[q], self.target1(q)).wait_send()

            for k in range(4):

                @pl.when(jnp.logical_not(self.is_self(self.target2(q, k))))
                def _():
                    self.copy(self.second(q, k, 0, 0), self.send2.at[q, k], self.target2(q, k)).wait_send()

            return carry

        lax.fori_loop(0, self.n, step, 0)

    def greet(self, greet):
        def step(q, count):
            ri, cq, s = self.source(q)
            source = ri, 4 * cq + s

            @pl.when(jnp.logical_not(self.is_self(source)))
            def _():
                greet(*source)

            count = count + jnp.logical_not(self.is_self(self.target1(q))).astype(jnp.int32)
            for k in range(4):
                relay = self.relay_of(self.cq, self.ri, k, q)

                @pl.when(jnp.logical_not(self.is_self(relay)))
                def _():
                    greet(*relay)

                away = jnp.logical_not(self.is_self(self.target2(q, k)))
                count = count + away.astype(jnp.int32)
            return count

        return lax.fori_loop(0, self.n, step, jnp.int32(0))

    def fetch(self):
        lane = lax.broadcasted_iota(jnp.int32, (8, BC, BR), 2)
        half = lane < 64
        even = (lane // 32) % 2 == 0
        l0, l1, l2, l3 = (self.land[k] for k in range(4))
        a0 = jnp.where(half, l0, pltpu.roll(l2, 64, 2))
        a2 = jnp.where(half, pltpu.roll(l0, 64, 2), l2)
        a1 = jnp.where(half, l1, pltpu.roll(l3, 64, 2))
        a3 = jnp.where(half, pltpu.roll(l1, 64, 2), l3)
        return (
            jnp.where(even, a0, pltpu.roll(a1, 32, 2)),
            jnp.where(even, pltpu.roll(a0, 96, 2), a1),
            jnp.where(even, a2, pltpu.roll(a3, 32, 2)),
            jnp.where(even, pltpu.roll(a2, 96, 2), a3),
        )


class Place:
    def __init__(self, nrow, ncol):
        self.nrow = nrow
        self.ncol = ncol
        self.ri = lax.axis_index("row")
        self.ci = lax.axis_index("col")

    def inside(self, dr, dc):
        ok = None
        for index, step, size in ((self.ri, dr, self.nrow), (self.ci, dc, self.ncol)):
            if step:
                here = index < size - 1 if step > 0 else index > 0
                ok = here if ok is None else ok & here
        return ok


def interleave(groups):
    return jnp.concatenate(groups, axis=1)


class Total:
    def __init__(self, place, refs):
        self.place = place
        self.acc, self.r1, self.mine, self.r2, self.fin = refs[:5]
        self.send1, self.recv1, self.send2, self.recv2, self.send3, self.recv3 = refs[5:]
        self.owners = self.acc.shape[0]
        self.n1 = place.ncol // 2
        self.n2 = 2 * place.nrow
        self.a = lax.rem(place.ci, self.n1)
        self.half = place.ci // self.n1
        self.m = place.ri * 2 + self.half
        self.owner = self.a < self.owners

    @staticmethod
    def scratch(n1, n2, owners, count):
        block = (count, 3 * C // owners, BR)
        vmem = pltpu.VMEM
        return [
            vmem((owners,) + block, F32),
            vmem((n1,) + block, F32),
            vmem(block, F32),
            vmem((n2,) + block, F32),
            vmem((owners,) + block, F32),
        ] + [pltpu.SemaphoreType.DMA((n,)) for n in (owners, n1, n2, n2, n1, owners)]

    def group1(self, b):
        return self.place.ri, self.half * self.n1 + b

    def group2(self, m):
        return m // 2, lax.rem(m, 2) * self.n1 + self.a

    def others(self, count, me, body):
        def step(b, carry):
            @pl.when(b != me)
            def _():
                body(b)

            return carry

        lax.fori_loop(0, count, step, 0)

    def share(self, src, dst, send, recv, device):
        return pltpu.make_async_remote_copy(
            src_ref=src, dst_ref=dst, send_sem=send, recv_sem=recv, device_id=device, device_id_type=MESH
        )

    def scatter(self, b, slot):
        return self.share(
            self.acc.at[b], self.r1.at[slot], self.send1.at[b], self.recv1.at[slot], self.group1(b)
        )

    def spread(self, m, slot):
        return self.share(
            self.mine, self.r2.at[slot], self.send2.at[m], self.recv2.at[slot], self.group2(m)
        )

    def gather(self, b, src, slot):
        return self.share(
            self.fin.at[src], self.fin.at[slot], self.send3.at[b], self.recv3.at[slot], self.group1(b)
        )

    def start1(self):
        self.others(self.owners, self.a, lambda b: self.scatter(b, self.a).start())

    def start2(self):
        @pl.when(self.owner)
        def _():
            self.r1[self.a] = self.acc[self.a]
            self.others(self.n1, self.a, lambda b: self.scatter(0, b).wait_recv())
            self.mine[...] = sum(self.r1[b] for b in range(self.n1))
            self.others(self.n2, self.m, lambda m: self.spread(m, self.m).start())
            self.r2[self.m] = self.mine[...]

    def start3(self):
        @pl.when(self.owner)
        def _():
            self.others(self.n2, self.m, lambda m: self.spread(m, m).wait_recv())
            self.fin[self.a] = sum(self.r2[m] for m in range(self.n2))
            self.others(self.n1, self.a, lambda b: self.gather(b, self.a, self.a).start())

    def finish(self):
        self.others(self.owners, self.a, lambda b: self.gather(0, 0, b).wait_recv())

    def drain(self):
        self.others(self.owners, self.a, lambda b: self.scatter(b, 0).wait_send())

        @pl.when(self.owner)
        def _():
            self.others(self.n2, self.m, lambda m: self.spread(m, 0).wait_send())
            self.others(self.n1, self.a, lambda b: self.gather(b, self.a, 0).wait_send())


def kernel_grad(padding, own, stacked, d, out, which):
    def fill(k):
        padding[k + 2 * d] = own(k)

    rows(BC, fill, 16)
    total = jnp.zeros((3 * C, 3 * C), F32)
    for t in range((BC + 2 * d) // 8):
        left = []
        right = []
        for k in range(t * 8, t * 8 + 8):
            left.append(
                jnp.concatenate([padding[k + 2 * d], padding[k + d], padding[k]], axis=0)
            )
            right.append(stacked[k, :, 0:BR])
        total = total + lax.dot_general(
            jnp.concatenate(left, axis=1),
            jnp.concatenate(right, axis=1),
            (((1,), (1,)), ((), ())),
            preferred_element_type=F32,
        )
    per = out.shape[2]
    for t in range(3 * C // per):
        out[t, which, :, 0 : 3 * C] = total[t * per : t * per + per]


def main_kernel(nrow, ncol, *refs):
    inputs, (dec_out, g0_out, early_out, late_out) = refs[:6], refs[6:10]
    rest = list(refs[10:])

    def take(n):
        out = rest[:n]
        del rest[:n]
        return out

    place = Place(nrow, ncol)
    ri, ci = place.ri, place.ci
    halo_x = Halo(8, place, take(7), True)
    halo_s2 = Halo(16, place, take(7), True)
    halo_z = Halo(16, place, take(7), True)
    halo_s1 = Halo(8, place, take(7))
    halos = (halo_x, halo_s2, halo_z, halo_s1)
    mir_g = Mirror(place, take(7))
    mir_y = Mirror(place, take(7))
    early = Total(place, take(11))
    late = Total(place, take(11))
    held = take(6)
    x_ref, g_ref, fa, fb, sa, sb = held
    in_sem, out_sem = take(2)
    (wa1, wb1, wa2, wb2, wb2t, tb2, ta2, ta2t, tb1, ta1) = take(10)
    (xc1, hc1, slope1, xc2, sc2, hg2, hc2, hc2t, ec2, ec2t, sc1, ec1, y1, dec, g0) = take(15)
    pad1, pad2, dec_nat, g0_nat = take(4)

    loads = [
        pltpu.make_async_copy(src, dst, in_sem.at[k]) for k, (src, dst) in enumerate(zip(inputs, held))
    ]
    for load in loads:
        load.start()

    barrier = pltpu.get_barrier_semaphore()
    expected = jnp.int32(early.n1 + early.n2 - 2)

    def greet(row, col):
        pl.semaphore_signal(barrier, inc=1, device_id=(row, col), device_id_type=MESH)

    for dr in (-1, 0, 1):
        for dc in (-1, 0, 1):
            if dr or dc:
                ok = place.inside(dr, dc)
                expected = expected + ok.astype(jnp.int32)

                @pl.when(ok)
                def _():
                    greet(ri + dr, ci + dc)

    expected = expected + mir_g.greet(greet)
    early.others(early.n1, early.a, lambda b: greet(*early.group1(b)))
    early.others(early.n2, early.m, lambda m: greet(*early.group2(m)))

    order = permutation(False)
    loads[0].wait()
    flat = x_ref[...].reshape(C * BC, BR)
    halo_x.own[...] = interleave(
        [dot(order, flat[256 * t : 256 * t + 256]).reshape(BC, 8, BR) for t in range(4)]
    ).astype(BF)
    halo_x.pack_sides()
    for load in loads[1:]:
        load.wait()
    gflat = g_ref[...].reshape(C * BC, BR)
    for j in range(8):
        mir_g.out[j] = gflat[j * BR : j * BR + BR].T
    fill_matrix(wa1, 0, fa, False, False)
    fill_matrix(wb1, 0, fb, False, False)
    pl.semaphore_wait(barrier, expected)
    halo_x.start()
    mir_g.start()

    fill_matrix(wa2, 0, sa, False, False)
    fill_matrix(wa2, C, sa, False, True)
    fill_matrix(wb2, 0, sb, False, False)
    fill_matrix(wb2t, 0, sb, False, True)
    fill_matrix(tb2, 0, sb, True, False)
    fill_matrix(tb2, C, sb, True, True)
    fill_matrix(ta2, 0, sa, True, False)
    fill_matrix(ta2t, 0, sa, True, True)
    fill_matrix(tb1, 0, fb, True, False)
    fill_matrix(ta1, 0, fa, True, False)
    for halo in halos:
        halo.fill_edges()
    for ref in (pad1, pad2, early.acc, late.acc):
        ref[...] = jnp.zeros(ref.shape, ref.dtype)

    lane = lax.broadcasted_iota(jnp.int32, (C, BR), 1)
    first_lane = jnp.where(ri < nrow - 1, 0, 64)
    last_lane = jnp.where(ri > 0, BR, 64)
    side_ok = (lane >= first_lane) & (lane < last_lane)

    def put_field(ref, k, d, v):
        bin_index = ci * BC + k - d
        ok = (bin_index >= 0) & (bin_index < ncol * BC)
        main = jnp.where(ok, v[:, :BR], 0.0).astype(BF)
        side = jnp.where(side_ok & ok, v[:, BR:], 0.0).astype(BF)
        put_stack(ref, k, main, side, d)

    d = DILATE_ONE
    halo_x.prepare(xc1, d)
    halo_x.forward()
    mir_g.forward()
    halo_x.build(xc1, d, outer=False)

    def hidden1(k):
        pre = dot(wa1[...], taps(xc1, k, d))
        sig = jax.nn.sigmoid(pre)
        slope1[k] = sig * (1.0 + pre * (1.0 - sig))
        put_field(hc1, k, d, pre * sig)

    rows(24, hidden1, 24, 8)
    halo_x.wait()
    halo_x.build(xc1, d, inner=False)

    def edge1(t, carry):
        for u in range(8):
            hidden1(t * 32 + u)
        return carry

    lax.fori_loop(0, 2, edge1, 0)

    def outer1(k):
        y1[k] = (halo_x.own[k].astype(F32) + dot(wb1[...], taps(hc1, k, d))).astype(BF)

    rows(BC, outer1, 16)

    back = permutation(True)
    for t in range(4):
        part = y1[:, 8 * t : 8 * t + 8, :].reshape(256, BR)
        natural = dot(back, part)
        for j in range(2):
            mir_y.out[2 * t + j] = natural[j * BR : j * BR + BR].T.astype(BF)
    mir_y.start()
    mir_y.forward()

    mir_g.wait()
    turned = mir_g.fetch()
    parts = []
    for t in range(4):
        mirrored = jnp.concatenate(
            [turned[n][2 * t + j] for j in range(2) for n in range(4)], axis=0
        )
        here = gflat[256 * t : 256 * t + 256]
        mean = ((here.astype(F32) + mirrored.astype(F32)) * 0.5).astype(BF)
        parts.append(dot(order, mean).reshape(BC, 8, BR))
    halo_s2.own[...] = interleave(parts).astype(BF)
    halo_s2.pack_sides()
    halo_s2.start()
    halo_s2.prepare(sc2, DILATE_TWO)

    mir_y.wait()
    turned = mir_y.fetch()
    parts = []
    for t in range(4):
        mirrored = jnp.concatenate(
            [turned[n][2 * t + j] for j in range(2) for n in range(4)], axis=0
        )
        parts.append(dot(order, mirrored).reshape(BC, 8, BR))
    halo_z.own[...] = ((y1[...].astype(F32) + interleave(parts)) * 0.5).astype(BF)
    halo_z.pack_sides()
    halo_z.start()
    halo_s2.forward()
    halo_s2.build(sc2, DILATE_TWO, outer=False)
    halo_z.prepare(xc2, DILATE_TWO)

    d = DILATE_TWO

    def cotangent2(k):
        hg2[k] = dot(tb2[...], taps(sc2, k, d))

    halo_s2.wait()
    halo_s2.build(sc2, d, inner=False)
    rows(BC + 2 * d, cotangent2, 16)
    halo_z.forward()
    halo_z.build(xc2, d, outer=False)

    def hidden2(k):
        pre = dot(wa2[...], taps(xc2, k, d))
        sig = jax.nn.sigmoid(pre)
        hid = pre * sig
        grad = hg2[k] * (sig * (1.0 + pre * (1.0 - sig)))
        hg2[k] = hid
        put_field(ec2, k, d, grad[:C])
        put_field(ec2t, k, d, grad[C:])

    rows(16, hidden2, 16, 16)
    halo_z.wait()
    halo_z.build(xc2, d, inner=False)
    outer_rows(hidden2, 16)

    def upstream1(k):
        base = halo_s2.own[k].astype(F32)
        one = (base + dot(ta2[...], taps(ec2, k, d))).astype(BF)
        two = (base + dot(ta2t[...], taps(ec2t, k, d))).astype(BF)
        halo_s1.own[k] = ((one.astype(F32) + two.astype(F32)) * 0.5).astype(BF)

    rows(BC, upstream1, 16)
    halo_s1.pack_sides()
    halo_s1.start()
    halo_s1.prepare(sc1, DILATE_ONE)

    def place2(k):
        put_field(hc2, k, DILATE_TWO, hg2[k, :C, :])

    rows(BC + 2 * d, place2)
    kernel_grad(pad2, lambda k: halo_s2.own[k], hc2, d, early.acc, 2)
    kernel_grad(
        pad2, lambda k: ec2[k + DILATE_TWO, C : 2 * C, :], xc2.at[d : d + BC + 2 * d], d, early.acc, 1
    )

    d = DILATE_ONE
    kernel_grad(pad1, lambda k: halo_s1.own[k], hc1, d, early.acc, 0)
    early.start1()
    halo_s1.wait()
    halo_s1.build(sc1, d)

    def cotangent1(k):
        put_field(ec1, k, d, dot(tb1[...], taps(sc1, k, d)) * slope1[k])

    rows(BC + 2 * d, cotangent1, 20)
    kernel_grad(
        pad1, lambda k: ec1[k + DILATE_ONE, C : 2 * C, :], xc1.at[d : d + BC + 2 * d], d, late.acc, 0
    )
    late.start1()
    early.start2()

    def by_channel(src, dst):
        for t in range(4):
            part = src[:, 8 * t : 8 * t + 8, :].reshape(256, BR)
            dst[8 * t : 8 * t + 8] = dot(back, part).astype(BF).reshape(8, BC, BR)

    def upstream0(k):
        g0[k] = (halo_s1.own[k].astype(F32) + dot(ta1[...], taps(ec1, k, d))).astype(BF)

    rows(BC, upstream0, 16)
    by_channel(g0, g0_nat)
    g0_copy = pltpu.make_async_copy(g0_nat, g0_out, out_sem.at[0])
    g0_copy.start()
    late.start2()

    def place2t(k):
        put_field(hc2t, k, DILATE_TWO, hg2[k, C:, :])

    rows(BC + 16, place2t)

    def outer2(k):
        base = halo_z.own[k].astype(F32)
        one = (base + dot(wb2[...], taps(hc2, k, DILATE_TWO))).astype(BF)
        two = (base + dot(wb2t[...], taps(hc2t, k, DILATE_TWO))).astype(BF)
        dec[k] = ((one.astype(F32) + two.astype(F32)) * 0.5).astype(BF)

    rows(BC, outer2, 16)
    by_channel(dec, dec_nat)
    dec_copy = pltpu.make_async_copy(dec_nat, dec_out, out_sem.at[1])
    dec_copy.start()
    early.start3()
    late.start3()
    for halo in halos:
        halo.drain()
    mir_g.drain()
    mir_y.drain()
    early.finish()
    early_copy = pltpu.make_async_copy(early.fin, early_out, out_sem.at[2])
    early_copy.start()
    late.finish()
    late_copy = pltpu.make_async_copy(late.fin, late_out, out_sem.at[3])
    late_copy.start()
    early.drain()
    late.drain()
    for copy in (g0_copy, dec_copy, early_copy, late_copy):
        copy.wait()


def finish_kernel(dec_in, g0_in, early_in, late_in, out_dec, out_g0, out_a1, out_b1, out_a2, out_b2, early, late, sems):
    copies = [
        pltpu.make_async_copy(src, dst, sems.at[k])
        for k, (src, dst) in enumerate(
            ((late_in, late), (early_in, early), (dec_in, out_dec), (g0_in, out_g0))
        )
    ]
    for copy in copies:
        copy.start()
    copies[0].wait()
    copies[1].wait()
    owners = early.shape[0]
    for src, which, dst in ((late, 0, out_a1), (early, 0, out_b1), (early, 1, out_a2), (early, 2, out_b2)):
        band = src[:, which].reshape(3 * C, BR)
        for p in range(3):
            for q in range(3):
                dst[p, q] = band[p * C : p * C + C, q * C : q * C + C]
    copies[2].wait()
    copies[3].wait()


def per_device(nrow, ncol, *arrays):
    n1 = ncol // 2
    n2 = 2 * nrow
    owners = 12 if n1 >= 12 else 4
    wide = BC + 16
    vmem = pltpu.VMEM
    grad_shapes = [(owners, count, 3 * C // owners, BR) for count in (3, 1)]
    scratch = (
        Halo.scratch(8)
        + Halo.scratch(16)
        + Halo.scratch(16)
        + Halo.scratch(8)
        + Mirror.scratch(nrow)
        + Mirror.scratch(nrow)
        + Total.scratch(n1, n2, owners, 3)
        + Total.scratch(n1, n2, owners, 1)
        + [vmem((C, BC, BR), BF)] * 2
        + [vmem((3, 3, C, C), BF)] * 4
        + [pltpu.SemaphoreType.DMA((6,)), pltpu.SemaphoreType.DMA((4,))]
        + [vmem((m, 9 * C), BF) for m in (C, C, 2 * C, C, C, 2 * C, C, C, C, C)]
        + [
            vmem((BC + 16, 3 * C, 2 * BR), BF),
            vmem((BC + 8, 3 * C, BR), BF),
            vmem((BC + 8, C, 2 * BR), F32),
            vmem((BC + 32, 3 * C, 2 * BR), BF),
            vmem((BC + 32, 3 * C, 2 * BR), BF),
            vmem((wide, 2 * C, 2 * BR), F32),
            vmem((wide, 3 * C, BR), BF),
            vmem((wide, 3 * C, BR), BF),
            vmem((wide, 3 * C, BR), BF),
            vmem((wide, 3 * C, BR), BF),
            vmem((BC + 16, 3 * C, 2 * BR), BF),
            vmem((BC + 8, 3 * C, BR), BF),
            vmem((BC, C, BR), BF),
            vmem((BC, C, BR), BF),
            vmem((BC, C, BR), BF),
            vmem((BC + 16, C, BR), BF),
            vmem((BC + 32, C, BR), BF),
            vmem((C, BC, BR), BF),
            vmem((C, BC, BR), BF),
        ]
    )
    whole = pl.BlockSpec(memory_space=pltpu.VMEM)
    anywhere = pl.BlockSpec(memory_space=pl.ANY)
    field = jax.ShapeDtypeStruct((C, BC, BR), BF)
    results = pl.pallas_call(
        functools.partial(main_kernel, nrow, ncol),
        out_shape=[field, field] + [jax.ShapeDtypeStruct(shape, F32) for shape in grad_shapes],
        in_specs=[anywhere] * 6,
        out_specs=[anywhere] * 4,
        scratch_shapes=scratch,
        compiler_params=pltpu.CompilerParams(
            collective_id=0, has_side_effects=True, vmem_limit_bytes=56 << 20
        ),
        name="blocks",
    )(*arrays)
    small = jax.ShapeDtypeStruct((3, 3, C, C), F32)
    return pl.pallas_call(
        finish_kernel,
        out_shape=[field, field, small, small, small, small],
        in_specs=[anywhere] * 4,
        out_specs=[whole] * 6,
        scratch_shapes=[vmem(shape, F32) for shape in grad_shapes]
        + [pltpu.SemaphoreType.DMA((4,))],
        compiler_params=pltpu.CompilerParams(vmem_limit_bytes=56 << 20),
        name="finish",
    )(*results)


def solution(mesh):
    return jax.shard_map(
        functools.partial(per_device, mesh.shape["row"], mesh.shape["col"]),
        mesh=mesh,
        in_specs=(P(None, "col", "row"), P(None, "col", "row"), P(), P(), P(), P()),
        out_specs=(P(None, "col", "row"), P(None, "col", "row"), P(), P(), P(), P()),
        check_vma=False,
    )
```
